512 devices in a mesh: row: 16 (over z_hi, y), col: 32 (over x, z_lo, core).
Axes of the slice: x: 4, y: 8, z: 8 (z_hi: 2, z_lo: 4; z = z_hi * 4 + z_lo), core: 2. Of those that a mesh axis runs over, the one named last changes fastest.
Arguments:
- cov_tiles: float32 [2, 16, 1, 32, 512, 512], P(None, 'row', None, 'col'), may hold values from -6 to 6
- inverse_factors: float32 [2, 512, 512], P(None, 'row'), may hold values from -0.3 to 0.3, as said below
- band: int32 [32], replicated, may hold values from 1 to 24, as said below
- station_noise: float32 [16384], replicated, may hold values from 0.5 to 4
- morton: int32 [16384], replicated, may hold values from 0 to 16383, each once
Outputs:
- factor_window: float32 [2, 16, 1, 32, 512, 512], P(None, 'row', None, 'col')
The draws below stay inside these ranges and needn't reach their ends.
Inputs may be any that keep to these rules, and one draw needn't show every extreme that they name: `inverse_factors`: each matrix is upper triangular with a positive diagonal. Some row of tiles has a band of exactly 24.
All inputs are finite; a program needn't handle non-finite values.
Results may differ from the reference program's by a relative error of at most 0.0003.
Values sent between devices are 32-bit elements; how exact they have to be, the bound alone decides.
A program may use at most 64 MiB of HBM per device.

```python
import math
import jax
import jax.numpy as jnp
from jax import lax

TILE = 512
BAND = 24
STEPS = 2
TC = 1
NT = 32
TR = 2
N = 16384
N_ROW = 16
N_COL = 32


def draw_inverse_factors(key, part):
    key = jax.random.fold_in(key, 11)
    first_key, second_key = jax.random.split(key)
    offsets = jnp.clip(jax.random.normal(first_key, (STEPS, TILE, TILE), jnp.float32), -6.0, 6.0)
    diagonal = jnp.exp(jax.random.uniform(second_key, (STEPS, TILE), jnp.float32, math.log(0.5), math.log(1.5)))
    upper_part = jnp.triu(offsets, 1) / math.sqrt(TILE)
    identity = jnp.eye(TILE, dtype=jnp.float32)
    return 0.15 * (upper_part + diagonal[:, None, :] * identity)


def draw_band(key, part):
    key = jax.random.fold_in(key, 5)
    first_key, second_key = jax.random.split(key)
    values = jax.random.randint(first_key, (NT,), 1, BAND + 1)
    widest = jax.random.randint(second_key, (), 0, NT)
    return jnp.where(jnp.arange(NT) == widest, BAND, values).astype(jnp.int32)


def block_scale(stream_key, shape, shards, smallest, top_value):
    gain = 1.0
    for dim, blocks in shards:
        draws = jax.random.uniform(jax.random.fold_in(jax.random.fold_in(stream_key, 6), dim), (blocks,), jnp.float32, smallest / len(shards), top_value / len(shards))
        gain = gain * jnp.repeat(jnp.exp(draws), shape[dim] // blocks).reshape((-1,) + (1,) * (len(shape) - 1 - dim))
    return gain


def gaussian(stream_key, shape, spread, bound, pieces=(), held_as=jnp.bfloat16):
    loudness = block_scale(stream_key, shape, pieces, -0.22, 0.18) if pieces else 1.0
    result = jax.random.normal(stream_key, shape, jnp.float32) * spread * loudness
    return jnp.minimum(jnp.maximum(result, -bound), bound).astype(held_as)


def setup_inputs(seed: int = 0) -> dict:
    keys = jax.random.split(jax.random.key(seed), 6)
    cov_tiles = gaussian(keys[0], (TR, N_ROW, TC, N_COL, TILE, TILE), 1.0, 6.0, ((1, 16), (3, 32)), jnp.float32)
    inverse_factors = draw_inverse_factors(jax.random.fold_in(keys[5], 71), 0)
    band = draw_band(jax.random.fold_in(keys[5], 71), 0)
    station_noise = jnp.clip(jnp.exp(jax.random.uniform(keys[3], (N,), jnp.float32, math.log(0.5), math.log(4.0))), 0.5, 4.0)
    morton = jax.random.permutation(keys[4], N).astype(jnp.int32)
    return dict(cov_tiles=cov_tiles, inverse_factors=inverse_factors, band=band, station_noise=station_noise, morton=morton)


def reference(cov_tiles, inverse_factors, band, station_noise, morton):
    tile_count = band.shape[0]
    tile_size = cov_tiles.shape[-1]
    matrix = cov_tiles.reshape(tile_count, tile_count, tile_size, tile_size)
    tile_index = jnp.arange(tile_count, dtype=jnp.int32)
    row_ids = tile_index[:, None]
    col_ids = tile_index[None, :]
    kept_mask = (col_ids <= row_ids) & (row_ids - col_ids <= band[:, None])
    matrix = jnp.where(kept_mask[:, :, None, None], matrix, 0.0)
    diagonal = matrix[tile_index, tile_index]
    mirrored = jnp.tril(diagonal) + jnp.swapaxes(jnp.tril(diagonal, -1), 1, 2)
    nugget = station_noise[morton].reshape(tile_count, tile_size)
    mirrored = mirrored + nugget[:, :, None] * jnp.eye(tile_size, dtype=mirrored.dtype)
    matrix = matrix.at[tile_index, tile_index].set(mirrored)
    for panel_step in range(STEPS):
        row_factor = jnp.einsum('imn,np->imp', matrix[:, panel_step], inverse_factors[panel_step],
                                precision=lax.Precision.HIGHEST)
        row_factor = jnp.where((tile_index > panel_step)[:, None, None], row_factor, 0.0)
        matrix = matrix.at[:, panel_step].set(row_factor)

        def one_row(packed):
            tile_row, row_left, row_id = packed
            update = jnp.einsum('mp,jnp->jmn', row_left, row_factor, precision=lax.Precision.HIGHEST)
            active = (tile_index > panel_step) & (tile_index <= row_id)
            return tile_row - jnp.where(active[:, None, None], update, 0.0)

        matrix = lax.map(one_row, (matrix, row_factor, tile_index))
    return matrix.reshape(TR, N_ROW, TC, N_COL, tile_size, tile_size)
```

```python
import jax
import jax.numpy as jnp
from jax import lax
from jax.experimental import pallas as pl
from jax.experimental.pallas import tpu as pltpu
from jax.sharding import PartitionSpec as P

TILE = 512
NP = 16
PIECE = 2 * TILE // NP
HALF = PIECE // 2
ROW_HOP = 2
COL_HOP = 2
DEEPEST = 9
STEPS = NP + ROW_HOP * DEEPEST + COL_HOP * 7 + 1
BLOCK = 128
MESH = pl.DeviceIdType.MESH
F32 = jnp.float32
BF16 = jnp.bfloat16


def device(x, y, z, core):
    x, y, z = lax.rem(x + 4, 4), lax.rem(y + 8, 8), lax.rem(z + 8, 8)
    return (z // 4 * 8 + y, x * 8 + z % 4 * 2 + core)


def split(value):
    high = value.astype(BF16)
    return high, (value - high.astype(F32)).astype(BF16)


def dot3(a, b, transposed):
    dims = (((1,), (1 if transposed else 0,)), ((), ()))

    def dot(p, q):
        return lax.dot_general(p, q, dims, preferred_element_type=F32)

    return dot(a[0], b[0]) + (dot(a[0], b[1]) + dot(a[1], b[0]))


def either(*conditions):
    result = conditions[0]
    for condition in conditions[1:]:
        result = result | condition
    return result


def count(*conditions):
    return sum(jnp.where(condition, 1, 0) for condition in conditions)


def kernel(cov, factors, band, noise, morton, out, buf, panel, fac, lead, wide, narrow,
           row_got, side_got, up_got, down_got, fac_got, lead_got, one_got,
           z_sent, xp_sent, xm_sent, side_sent, cross_sent, up_sent, down_sent, fac_sent, lead_sent, spread_sent, one_sent):
    row = lax.axis_index("row")
    col = lax.axis_index("col")
    half, y = row // 8, row % 8
    x, zl, core = col // 8, col % 8 // 2, col % 2
    z = half * 4 + zl
    other = 1 - core
    sibling = device(x, y, z, other)
    home = (x == 0) & (zl == 0)
    first, second = core == 0, core == 1
    low, high = half == 0, half == 1
    tail = high & (y <= 1)

    z_child = (zl < 3) & either(first & (x == 0), second & low & (x == 1), second & tail & (x == 2))
    xp_child = either(first & high & (x == 0), second & low & either(x == 1, home))
    xm_child = either(second & low & (x == 1) & (zl >= 1),
                      second & tail & either(home, (x == 3) & (zl == 0), x == 2, (x == 1) & (zl >= 1)))
    from_z = (zl >= 1) & either(first & (x == 0), second & low & (x == 1), second & tail & (x == 2))
    from_xm = either(first & high & (x == 1), second & low & either(x == 2, (x == 1) & (zl == 0)))
    from_xp = either(second & low & (x == 0) & (zl >= 1),
                     second & tail & either((x == 3) & (zl == 0), (x == 2) & (zl == 0), x == 1, (x == 0) & (zl >= 1)))
    row_in = either(from_z, from_xm, from_xp)
    has_row = home | row_in
    side_in = home | either(second & ((x == 0) | (high & (x == 1))),
                            first & low & (x <= 2),
                            first & tail & ((x <= 2) | (zl == 0)))
    depth_low = jnp.where(x == 1, zl + 1, zl + 2)
    depth_tail = jnp.where(x == 3, 1, zl + jnp.where(x == 2, 2, jnp.where(x == 1, 3, 4)))
    depth = jnp.where(home, 0, jnp.where(first, zl + x, jnp.where(low, depth_low, depth_tail)))

    place = lax.rem(y - 2 * zl - core + 8, 8)
    ring = (x <= 2) & jnp.logical_not(home)
    source = ring & (place == 0)
    follower = ring & (place >= 1)
    own_row = source & either((x == half), (x == 2) & low)
    crossed = source & jnp.logical_not(own_row)
    last = (x == 3) & (zl == 0) & high & first
    last_source, last_follower = last & (y == 0), last & (y == 1)
    slot = jnp.where(x >= 2, 1, 0)
    by_side = (own_row & (slot != core)) | last_source
    lag = jnp.where(x == 3, 3,
                    jnp.where(x == 2, zl + 3 + 2 * half,
                              jnp.where(x == half, zl + x + core, 2)))
    held = jnp.where(either(own_row, (x == 3) & (zl == 0) & high & jnp.logical_not(last_follower)), slot, 2)
    cross_out = home & first & jnp.logical_not(low & (y < 2))
    jump_out = (x == 2) & low & (place == 0)
    jump_in = (x == 2) & high & (place == 0)
    cross_in = crossed & (x <= 1)
    send_up = (ring & (place <= 6))
    send_down = (ring & (place != 1))

    fac_own = home & first
    fac_far = (x == 0) & (zl == 3) & second
    fac_next = (x == 1) & (zl == 0) & first
    fac_off = (x == 3) & (zl == 3) & second
    scatter = home & low & (y == 1) & first
    relay = low & (y == 1) & (core == zl % 2)
    relay_place = zl % 2 * 8 + x * 2 + zl // 2

    barrier = pltpu.get_barrier_semaphore()

    def greet(target):
        pl.semaphore_signal(barrier, inc=1, device_id=target, device_id_type=MESH)

    def greet_if(condition, target):
        @pl.when(condition)
        def _():
            greet(target)

    greet(sibling)

    @pl.when(home)
    def _():
        for step in range(8):
            @pl.when(first)
            def _():
                @pl.when(y != step)
                def _():
                    greet(device(0, step, z, 0))

                greet(device(1, step, z, 0))

            @pl.when(second)
            def _():
                greet(device(0, step, z + 7, 1))
                greet(device(3, step, z + 7, 1))

            @pl.when(jnp.logical_not(scatter & (step == 0)))
            def _():
                greet(device(step // 2, 1, step % 2 * 2 + core, core))

    greet_if(relay & jnp.logical_not(scatter), device(0, 1, 0, 0))
    greet_if(from_z, device(x, y, z + 7, core))
    greet_if(from_xm, device(x + 3, y, z, core))
    greet_if(from_xp, device(x + 1, y, z, core))
    greet_if(follower, device(x, y + 7, z, core))
    greet_if(follower, device(x, y + 1, z, core))
    greet_if(last_follower, device(x, y + 7, z, core))
    greet_if(cross_in, device(0, y, 4 - 4 * half, 0))
    greet_if(jump_in, device(2, y, zl, core))
    targets = 1 + count(z_child, xp_child, xm_child, send_up, send_down, last_source, cross_out, jump_out)
    targets = targets + 7 * count(fac_own) + 8 * count(fac_far, fac_next, fac_off)
    targets = targets + 16 * count(relay) + 14 * count(scatter)
    pl.semaphore_wait(barrier, targets)

    def remote(src, dst, sent, got, target):
        return pltpu.make_async_remote_copy(
            src_ref=src, dst_ref=dst, send_sem=sent, recv_sem=got, device_id=target, device_id_type=MESH
        )

    chunk = TILE // 16

    def fac_rows(source_row):
        return pl.ds(pl.multiple_of(source_row * chunk, chunk), chunk)

    def fac_copy(part, step, target):
        return remote(factors.at[part], fac.at[part, fac_rows(row)], fac_sent.at[step], fac_got.at[part, y], target)

    def send_factors(condition, part, target_x, target_z, target_core, skip_self):
        @pl.when(condition)
        def _():
            for step in range(8):
                target = device(target_x, step, target_z, target_core)
                if skip_self:
                    @pl.when(y != step)
                    def _():
                        fac_copy(part, step, target).start()
                else:
                    fac_copy(part, step, target).start()

    def drain_factors(condition, part, skip_self):
        @pl.when(condition)
        def _():
            for step in range(8):
                if skip_self:
                    @pl.when(y != step)
                    def _():
                        fac_copy(part, step, sibling).wait_send()
                else:
                    fac_copy(part, step, sibling).wait_send()

    send_factors(fac_own, 0, 0, z, 0, True)
    send_factors(fac_far, 0, 0, z + 1, 1, False)
    side_panel = remote(cov.at[other], panel.at[core], one_sent.at[0], one_got.at[0], sibling)

    def lead_rows(number):
        return pl.ds(pl.multiple_of(number * chunk, chunk), chunk)

    def scatter_copy(number):
        parity, sx, sz = number // 8, number % 8 // 2, number % 2
        rows = pl.ds(number * chunk, chunk)
        return remote(cov.at[0, rows], lead.at[rows], spread_sent.at[number], one_got.at[4],
                      device(sx, 1, sz * 2 + parity, parity))

    @pl.when(scatter)
    def _():
        for number in range(1, 16):
            scatter_copy(number).start()
        lead[pl.ds(0, chunk)] = cov[0, pl.ds(0, chunk)]

    @pl.when(home)
    def _():
        side_panel.start()

    send_factors(fac_next, 1, 0, z, 0, False)
    send_factors(fac_off, 1, 0, z + 1, 1, False)

    def lead_copy(number, target):
        rows = lead_rows(relay_place)
        return remote(lead.at[rows], lead.at[rows], lead_sent.at[number], lead_got.at[relay_place % 8], target)

    @pl.when(relay)
    def _():
        rows = lead_rows(relay_place)

        @pl.when(jnp.logical_not(scatter))
        def _():
            remote(lead.at[rows], lead.at[rows], one_sent.at[4], one_got.at[4], sibling).wait_recv()

        for number in range(16):
            @pl.when(jnp.logical_not(scatter & (number == 1)))
            def _():
                lead_copy(number, device(0, number % 8, number // 8 * 4, core)).start()

    side_fac = [
        remote(fac.at[part, pl.ds(pl.multiple_of(jnp.where(first, half, 1 - half) * 256, 256), 256)],
               fac.at[part, pl.ds(pl.multiple_of(jnp.where(first, half, 1 - half) * 256, 256), 256)],
               one_sent.at[1 + part], one_got.at[1 + part], sibling)
        for part in range(2)
    ]
    side_lead_rows = pl.ds(pl.multiple_of(core * 256, 256), 256)
    side_lead = remote(lead.at[side_lead_rows], lead.at[side_lead_rows], one_sent.at[3], one_got.at[3], sibling)

    def wait_factors(part):
        own = jnp.where(first, half, 1 - half)
        if part == 0:
            @pl.when(first)
            def _():
                fac[0, fac_rows(row)] = factors[0]

        for step in range(8):
            def wait(step=step):
                remote(factors.at[part], fac.at[part, fac_rows(own * 8 + step)], fac_sent.at[step],
                       fac_got.at[part, step], sibling).wait_recv()

            if part == 0:
                pl.when(jnp.logical_not(first & (y == step)))(wait)
            else:
                wait()
        side_fac[part].start()

    def wait_lead():
        for step in range(8):
            @pl.when(jnp.logical_not(scatter & (step == 0)))
            def _():
                rows = lead_rows(core * 8 + step)
                remote(lead.at[rows], lead.at[rows], lead_sent.at[step], lead_got.at[step], sibling).wait_recv()
        side_lead.start()

    blocks = TILE // BLOCK

    def block_rows(number, start=0):
        return pl.ds(pl.multiple_of(start + number * BLOCK, BLOCK), BLOCK)

    def split_into(place, load):
        def body(number, carry):
            rows = block_rows(number)
            wide[place, rows], narrow[place, rows] = split(load(rows))
            return carry

        lax.fori_loop(0, blocks, body, 0)

    tile_row = core * 16 + row
    row_band = band[tile_row]

    def make_first():
        wait_factors(0)
        side_panel.wait_recv()

        @pl.when(first)
        def _():
            panel[0] = cov[0]

        @pl.when(second)
        def _():
            panel[1] = cov[1]

        side_fac[0].wait_recv()
        split_into(0, lambda rows: fac[0, rows])
        kept = (tile_row > 0) & (tile_row <= row_band)

        def body(number, carry):
            rows = block_rows(number)
            left = split(jnp.where(kept, panel[0, rows], 0.0))
            buf[core, rows] = dot3(left, (wide[0], narrow[0]), False)
            return carry

        lax.fori_loop(0, blocks, body, 0)

    def make_second():
        wait_factors(1)
        wait_lead()
        side_fac[1].wait_recv()
        side_lead.wait_recv()
        split_into(2, lambda rows: fac[1, rows])
        lead_kept = band[1] >= 1

        def body_lead(number, carry):
            rows = block_rows(number)
            left = split(jnp.where(lead_kept, lead[rows], 0.0))
            wide[1, rows], narrow[1, rows] = split(dot3(left, (wide[0], narrow[0]), False))
            return carry

        lax.fori_loop(0, blocks, body_lead, 0)
        kept = (tile_row > 0) & (tile_row - 1 <= row_band)

        def body(number, carry):
            rows = block_rows(number)
            update = dot3(split(buf[core, rows]), (wide[1], narrow[1]), True)
            left = split(jnp.where(kept, panel[1, rows], 0.0) - update)
            made = dot3(left, (wide[2], narrow[2]), False)
            buf[core, block_rows(number, TILE)] = jnp.where(tile_row > 1, made, 0.0)
            return carry

        lax.fori_loop(0, blocks, body, 0)

    def make_base():
        diagonal = row == lax.rem(col, 16)
        for s in range(2):
            tile = s * 16 + row
            kept = (col <= tile) & (tile - col <= band[tile])
            on_diagonal = diagonal & (col // 16 == s)

            @pl.when(on_diagonal)
            def _():
                stations = morton[pl.ds(tile, 1), :]
                upper, lower = stations // 128, stations % 128
                lanes = lax.broadcasted_iota(jnp.int32, (128, TILE), 0)
                pick = jnp.where(lanes == upper, 1.0, 0.0).astype(BF16)
                values = noise[...].T
                top = values.astype(BF16)
                rest = values - top.astype(F32)
                middle = rest.astype(BF16)
                bottom = (rest - middle.astype(F32)).astype(BF16)
                found = jnp.dot(top, pick, preferred_element_type=F32)
                found = found + (jnp.dot(middle, pick, preferred_element_type=F32)
                                 + jnp.dot(bottom, pick, preferred_element_type=F32))
                nugget = jnp.sum(jnp.where(lanes == lower, found, 0.0), axis=0, keepdims=True)
                for number in range(blocks):
                    at = number * BLOCK
                    rows_at = lax.broadcasted_iota(jnp.int32, (BLOCK, TILE), 0) + at
                    cols_at = lax.broadcasted_iota(jnp.int32, (BLOCK, TILE), 1)
                    here = cov[s, pl.ds(at, BLOCK), :]
                    turned = cov[s, :, pl.ds(at, BLOCK)].T
                    value = jnp.where(cols_at <= rows_at, here, turned)
                    out[s, pl.ds(at, BLOCK), :] = value + jnp.where(rows_at == cols_at, nugget, 0.0)

            @pl.when(jnp.logical_not(on_diagonal))
            def _():
                def body(number, carry):
                    rows = block_rows(number)
                    out[s, rows] = jnp.where(kept, cov[s, rows], 0.0)
                    return carry

                lax.fori_loop(0, blocks, body, 0)

    pl.when(home)(make_first)
    pl.when(jnp.logical_not(home))(make_base)

    def piece(index):
        return pl.ds(pl.multiple_of(index * PIECE, PIECE), PIECE)

    def half_piece(index, which):
        return pl.ds(pl.multiple_of(index * PIECE + which * HALF, HALF), HALF)

    def row_copy(index, sent, target):
        rows = piece(index)
        return remote(buf.at[core, rows], buf.at[core, rows], sent.at[index], row_got.at[index], target)

    def side_copy(index):
        rows = piece(index)
        return remote(buf.at[core, rows], buf.at[core, rows], side_sent.at[index], side_got.at[index], sibling)

    def side_arrival(index):
        rows = piece(index)
        return remote(buf.at[other, rows], buf.at[other, rows], side_sent.at[index], side_got.at[index], sibling)

    def whole_copy(index, from_slot, sent, target):
        rows = piece(index)
        return remote(buf.at[from_slot, rows], buf.at[2, rows], sent.at[index], up_got.at[index], target)

    def ring_copy(index, which, sent, got, target):
        rows = half_piece(index, which)
        return remote(buf.at[held, rows], buf.at[2, rows], sent.at[index], got.at[index], target)

    z_to, xp_to, xm_to = device(x, y, z + 1, core), device(x + 1, y, z, core), device(x + 3, y, z, core)
    up_to, down_to = device(x, y + 1, z, core), device(x, y + 7, z, core)
    cross_to = device(half, y, (1 - half) * 4 + y // 2, y % 2)
    jump_to = device(2, y, 4 + zl, core)
    row_delay = depth * ROW_HOP
    col_delay = lag * ROW_HOP

    def inside(index):
        return (index >= 0) & (index < NP)

    def step(time, carry):
        index = time - row_delay

        @pl.when(has_row & inside(index))
        def _():
            pl.when(home & (index == NP // 2))(make_second)

            @pl.when(row_in)
            def _():
                row_copy(index, z_sent, z_to).wait_recv()

            @pl.when(z_child)
            def _():
                row_copy(index, z_sent, z_to).start()

            @pl.when(xp_child)
            def _():
                row_copy(index, xp_sent, xp_to).start()

            @pl.when(xm_child)
            def _():
                row_copy(index, xm_sent, xm_to).start()

            @pl.when(cross_out)
            def _():
                whole_copy(index, 0, cross_sent, cross_to).start()

            side_copy(index).start()

        ahead = time - col_delay

        @pl.when((source | last_source) & inside(ahead))
        def _():
            @pl.when(by_side)
            def _():
                side_arrival(ahead).wait_recv()

            @pl.when(crossed)
            def _():
                whole_copy(ahead, 2, up_sent, up_to).wait_recv()

            @pl.when(source)
            def _():
                ring_copy(ahead, 0, up_sent, up_got, up_to).start()
                ring_copy(ahead, 1, down_sent, down_got, down_to).start()

            @pl.when(jump_out)
            def _():
                whole_copy(ahead, 1, cross_sent, jump_to).start()

            @pl.when(last_source)
            def _():
                whole_copy(ahead, 1, up_sent, up_to).start()

        going_up = ahead - COL_HOP * place
        going_down = ahead - COL_HOP * (8 - place)

        @pl.when(follower & inside(going_up))
        def _():
            copy = ring_copy(going_up, 0, up_sent, up_got, up_to)
            copy.wait_recv()

            @pl.when(place <= 6)
            def _():
                copy.start()

        @pl.when(follower & inside(going_down))
        def _():
            copy = ring_copy(going_down, 1, down_sent, down_got, down_to)
            copy.wait_recv()

            @pl.when(place >= 2)
            def _():
                copy.start()

        return carry

    lax.fori_loop(0, STEPS, step, 0)

    def finish(index, carry):
        @pl.when(side_in & jnp.logical_not(by_side))
        def _():
            side_arrival(index).wait_recv()

        @pl.when(last_follower)
        def _():
            whole_copy(index, 2, up_sent, up_to).wait_recv()

        return carry

    lax.fori_loop(0, NP, finish, 0)

    @pl.when(home)
    def _():
        for s in range(2):
            def body(number, carry):
                rows = block_rows(number)
                out[s, rows] = buf[s, block_rows(number, core * TILE)]
                return carry

            lax.fori_loop(0, blocks, body, 0)

    needed = [jnp.logical_not(home) & (col <= s * 16 + row) & (s * 16 + row <= 25) for s in range(2)]

    @pl.when(needed[0] | needed[1])
    def _():
        for part in range(2):
            split_into(part, lambda rows: buf[held, pl.ds(pl.multiple_of(rows.start + part * TILE, BLOCK), BLOCK)])
        for s in range(2):
            @pl.when(needed[s])
            def _():
                def body(number, carry):
                    rows = block_rows(number)
                    total = out[s, rows]
                    for part in range(2):
                        left = split(buf[s, block_rows(number, part * TILE)])
                        total = total - dot3(left, (wide[part], narrow[part]), True)
                    out[s, rows] = total
                    return carry

                lax.fori_loop(0, blocks, body, 0)

    def drain(index, carry):
        @pl.when(z_child)
        def _():
            row_copy(index, z_sent, z_to).wait_send()

        @pl.when(xp_child)
        def _():
            row_copy(index, xp_sent, xp_to).wait_send()

        @pl.when(xm_child)
        def _():
            row_copy(index, xm_sent, xm_to).wait_send()

        @pl.when(has_row)
        def _():
            side_copy(index).wait_send()

        @pl.when(cross_out | jump_out)
        def _():
            whole_copy(index, 2, cross_sent, cross_to).wait_send()

        @pl.when(last_source)
        def _():
            whole_copy(index, 1, up_sent, up_to).wait_send()

        @pl.when(send_up)
        def _():
            ring_copy(index, 0, up_sent, up_got, up_to).wait_send()

        @pl.when(send_down)
        def _():
            ring_copy(index, 1, down_sent, down_got, down_to).wait_send()

        return carry

    lax.fori_loop(0, NP, drain, 0)
    drain_factors(fac_own, 0, True)
    drain_factors(fac_far, 0, False)
    drain_factors(fac_next, 1, False)
    drain_factors(fac_off, 1, False)

    @pl.when(scatter)
    def _():
        for number in range(1, 16):
            scatter_copy(number).wait_send()

    @pl.when(relay)
    def _():
        for number in range(16):
            @pl.when(jnp.logical_not(scatter & (number == 1)))
            def _():
                lead_copy(number, sibling).wait_send()

    @pl.when(home)
    def _():
        side_panel.wait_send()
        side_fac[0].wait_send()
        side_fac[1].wait_send()
        side_lead.wait_send()


def on_device(cov_tiles, inverse_factors, band, station_noise, morton):
    vmem = pl.BlockSpec(memory_space=pltpu.VMEM)
    smem = pl.BlockSpec(memory_space=pltpu.SMEM)
    dma = pltpu.SemaphoreType.DMA
    out = pl.pallas_call(
        kernel,
        out_shape=jax.ShapeDtypeStruct((2, TILE, TILE), F32),
        in_specs=[vmem, vmem, smem, vmem, vmem],
        out_specs=vmem,
        scratch_shapes=[
            pltpu.VMEM((3, 2 * TILE, TILE), F32),
            pltpu.VMEM((2, TILE, TILE), F32),
            pltpu.VMEM((2, TILE, TILE), F32),
            pltpu.VMEM((TILE, TILE), F32),
            pltpu.VMEM((3, TILE, TILE), BF16),
            pltpu.VMEM((3, TILE, TILE), BF16),
            dma((NP,)), dma((NP,)), dma((NP,)), dma((NP,)), dma((2, 8)), dma((8,)), dma((5,)),
            dma((NP,)), dma((NP,)), dma((NP,)), dma((NP,)), dma((NP,)), dma((NP,)), dma((NP,)),
            dma((8,)), dma((16,)), dma((16,)), dma((5,)),
        ],
        compiler_params=pltpu.CompilerParams(
            collective_id=0, has_side_effects=True, vmem_limit_bytes=40 * 1024 * 1024
        ),
        cost_estimate=pl.CostEstimate(flops=6 * 4 * 2 * TILE**3, bytes_accessed=4 * 1024 * 1024, transcendentals=0),
        name="panel_steps",
    )(
        cov_tiles.reshape(2, TILE, TILE),
        inverse_factors,
        band,
        station_noise.reshape(128, 128),
        morton.reshape(32, TILE),
    )
    return out.reshape(cov_tiles.shape)


def solution(mesh):
    placed = (P(None, "row", None, "col", None, None), P(None, "row", None), P(), P(), P())
    return jax.shard_map(
        on_device,
        mesh=mesh,
        in_specs=placed,
        out_specs=P(None, "row", None, "col", None, None),
        check_vma=False,
    )
```

```python
import jax
import jax.numpy as jnp
from jax import lax
from jax.experimental import pallas as pl
from jax.experimental.pallas import tpu as pltpu
from jax.sharding import PartitionSpec as P

TILE = 512
BLOCK = 128
BLOCKS = TILE // BLOCK
NP = 32
PIECE = 2 * TILE // NP
HALF = PIECE // 2
GROUP = BLOCK // PIECE
ROW_HOP = 4
COL_HOP = 4
CHUNK = TILE // 16
MESH = pl.DeviceIdType.MESH
F32 = jnp.float32
BF16 = jnp.bfloat16


def device(x, y, z, core):
    x, y, z = lax.rem(x + 4, 4), lax.rem(y + 8, 8), lax.rem(z + 8, 8)
    return (z // 4 * 8 + y, x * 8 + z % 4 * 2 + core)


def split(value):
    high = value.astype(BF16)
    return high, (value - high.astype(F32)).astype(BF16)


def dot3(a, b, transposed):
    dims = (((1,), (1 if transposed else 0,)), ((), ()))

    def dot(p, q):
        return lax.dot_general(p, q, dims, preferred_element_type=F32)

    return dot(a[0], b[0]) + (dot(a[0], b[1]) + dot(a[1], b[0]))


def either(*conditions):
    result = conditions[0]
    for condition in conditions[1:]:
        result = result | condition
    return result


def count(*conditions):
    return sum(jnp.where(condition, 1, 0) for condition in conditions)


def kernel(cov, factors, band_in, noise_in, morton_in, out, buf, panel, fac, lead, wide, narrow, band, noise, morton,
           row_got, up_got, down_got, side_got, fac_got, lead_got, one_got,
           z_sent, xp_sent, xm_sent, cross_sent, direct_sent, up_sent, down_sent, side_sent, fac_sent, lead_sent, one_sent,
           local):
    row = lax.axis_index("row")
    col = lax.axis_index("col")
    half, y = row // 8, row % 8
    x, zl, core = col // 8, col % 8 // 2, col % 2
    z = half * 4 + zl
    other = 1 - core
    sibling = device(x, y, z, other)
    home = (x == 0) & (zl == 0)
    away = jnp.logical_not(home)
    first, second = core == 0, core == 1
    low, high = half == 0, half == 1
    tail = high & (y <= 1)
    turn, turn_core = y // 2, y % 2

    back = first & low & (x == 0) & (zl >= 1) & (zl < turn)
    from_below = (zl >= 1) & either(first & high & (x == 0), second & low & (x == 1), second & tail & (x == 2))
    from_xm = either(first & high & (x == 1) & (zl <= turn), second & low & either(x == 2, (x == 1) & (zl == 0)))
    from_xp = either(second & low & (x == 0) & (zl >= 1), second & low & (x == 3) & (zl == 0),
                     second & tail & either((x == 3) & (zl == 0), (x == 2) & (zl == 0), x == 1, (x == 0) & (zl >= 1)))
    row_in = either(back, from_below, from_xm, from_xp)
    z_child = either((zl < 3) & either(first & high & (x == 0), second & low & (x == 1), second & tail & (x == 2)),
                     back & (zl >= 2))
    xp_child = either(first & high & (x == 0) & (zl <= turn), second & low & either(x == 1, home))
    xm_child = either(second & low & either((x == 1) & (zl >= 1), home),
                      second & tail & either(home, (x == 3) & (zl == 0), x == 2, (x == 1) & (zl >= 1)))
    side_out = row_in & jnp.logical_not((x == 3) & low)
    depth_low = jnp.where((x == 1) | (x == 3), zl + 1, zl + 2)
    depth_tail = jnp.where(x == 3, 1, zl + jnp.where(x == 2, 2, jnp.where(x == 1, 3, 4)))
    depths = jnp.where(low, turn - zl + 1, zl + x), jnp.where(low, depth_low, depth_tail)
    depth = jnp.where(first, depths[0], depths[1])

    place = lax.rem(y - 2 * zl - core + 8, 8)
    here = place == 0
    ring = away & (x <= 2)
    source = ring & here
    follower = ring & jnp.logical_not(here)
    turning = source & (x == 0) & low
    own_row = (x == 1) & high & (zl == 0) & (y == 0) & first
    last_out = (x == 3) & (zl == 0) & high & (y == 0) & second
    last_in = (x == 3) & (zl == 0) & high & (y == 1) & first
    last_own = (x == 3) & (zl == 0) & tail & jnp.logical_not(last_in)
    lag = jnp.where(x == 0, 1, jnp.where((x == 1) & low, jnp.where(zl == 0, 2, 1),
                                          jnp.where((x == 2) & high & (zl == 0), 3, 2)))
    held = jnp.where(turning | own_row, 0, jnp.where(last_own, 1, 2))
    send_up = ring & (place <= 6)
    send_down = ring & (place != 1)

    turn_out = home & first & low & (y >= 2)
    cross_home = home & first & (y >= 2)
    cross_near = (x == 1) & (zl == 0) & tail & first
    feed_row = (x == 1) & (zl == 0) & high & first & (y >= 1)
    feed_far = (x == 3) & (zl == 0) & low & second
    direct_out = feed_row | feed_far | last_out
    cross_out = cross_near | (feed_far & (y >= 2))
    jump_out = source & (x == 2) & low & (zl == 0)
    direct_x = jnp.where(last_out, 3, jnp.where(feed_far, 2, 1))
    direct_to = device(direct_x, jnp.where(last_out, 1, y), half * 4 + jnp.where(last_out, 0, turn),
                       jnp.where(last_out, 0, turn_core))
    cross_to = device(jnp.where(feed_far, 2, half), y, (1 - half) * 4 + turn, turn_core)

    fac_own = home & first
    fac_far = (x == 0) & (zl == 3) & second
    fac_next = (x == 1) & (zl == 0) & first
    fac_off = (x == 3) & (zl == 3) & second
    scatter = home & low & (y == 1) & first
    relay = (y == 1) & either(first & ((z == 0) | (z == 7)), second & ((z == 1) | (z == jnp.where(x % 2 == 0, 2, 6))))
    relay_place = core * 8 + x + jnp.where(z == core, 0, 4)

    def relay_chip(number):
        at, near = number % 4, number % 8 < 4
        if number < 8:
            return at, 0 if near else 7
        return at, 1 if near else 2 + 4 * (at % 2)

    def local_copy(number, src, dst):
        return pltpu.make_async_copy(src, dst, local.at[number])

    band_copy = local_copy(0, band_in, band)
    noise_copy = local_copy(1, noise_in, noise)
    morton_copy = local_copy(2, morton_in, morton)
    cov_copy = local_copy(3, cov, out)
    panel_copy = local_copy(4, cov.at[core], panel.at[core])
    band_copy.start()

    @pl.when(home)
    def _():
        panel_copy.start()

    @pl.when(away)
    def _():
        noise_copy.start()
        morton_copy.start()
        cov_copy.start()

    barrier = pltpu.get_barrier_semaphore()

    def greet(target):
        pl.semaphore_signal(barrier, inc=1, device_id=target, device_id_type=MESH)

    def greet_if(condition, target):
        @pl.when(condition)
        def _():
            greet(target)

    greet(sibling)

    @pl.when(home)
    def _():
        for step in range(8):
            @pl.when(first)
            def _():
                @pl.when(y != step)
                def _():
                    greet(device(0, step, z, 0))

                greet(device(1, step, z, 0))

                @pl.when(jnp.logical_not(scatter & (step == 0)))
                def _():
                    at, level = relay_chip(step)
                    greet(device(at, 1, level, 0))

            @pl.when(second)
            def _():
                greet(device(0, step, z + 7, 1))
                greet(device(3, step, z + 7, 1))
                at, level = relay_chip(8 + step)
                greet(device(at, 1, level, 1))

    greet_if(relay & jnp.logical_not(scatter), device(0, 1, 0, 0))
    greet_if(back, device(0, y, z + 1, jnp.where(zl + 1 == turn, turn_core, 0)))
    greet_if(from_below, device(x, y, z + 7, core))
    greet_if(from_xm, device(x + 3, y, z, core))
    greet_if(from_xp, device(x + 1, y, z, core))
    greet_if(follower, device(x, y + 7, z, core))
    greet_if(follower, device(x, y + 1, z, core))
    greet_if(turning, device(0, y, 0, 0))
    greet_if(source & (x == 0) & high, device(0, y, 0, 0))
    greet_if(source & (x == 1) & low, device(jnp.where(zl == 0, 1, 0), y, 4, 0))
    greet_if(source & (x == 1) & high & jnp.logical_not(own_row), device(1, y, 4, 0))
    jump_in = source & (x == 2) & high & (zl == 0)
    greet_if(source & (x == 2) & jnp.logical_not(jump_in), device(3, y, 0, 1))
    greet_if(jump_in, device(2, y, 0, core))
    greet_if(last_in, device(3, 0, 4, 1))
    targets = 1 + count(z_child, xp_child, xm_child, send_up, send_down, turn_out, cross_home, direct_out, cross_out, jump_out,
                        turning & (zl >= 2))
    targets = targets + 7 * count(fac_own) + 8 * count(fac_far, fac_next, fac_off)
    targets = targets + 16 * count(relay) + 14 * count(scatter)
    pl.semaphore_wait(barrier, targets)

    def remote(src, dst, sent, got, target):
        return pltpu.make_async_remote_copy(
            src_ref=src, dst_ref=dst, send_sem=sent, recv_sem=got, device_id=target, device_id_type=MESH
        )

    def total(rows, sent, got):
        return remote(buf.at[0, pl.ds(0, rows)], buf.at[0, pl.ds(0, rows)], sent, got, sibling)

    def chunk_rows(number):
        return pl.ds(pl.multiple_of(number * CHUNK, CHUNK), CHUNK)

    def send_factors(condition, part, target_z, target_core, skip_self):
        @pl.when(condition)
        def _():
            for step in range(8):
                copy = remote(factors.at[part], fac.at[part, chunk_rows(row)], fac_sent, fac_got.at[part],
                              device(0, step, target_z, target_core))
                pl.when(y != step if skip_self else step >= 0)(copy.start)

    own_factor = local_copy(5, factors.at[0], fac.at[0, chunk_rows(row)])
    pl.when(fac_own)(own_factor.start)
    send_factors(fac_own, 0, z, 0, True)
    send_factors(fac_far, 0, z + 1, 1, False)

    own_lead = local_copy(6, cov.at[0, pl.ds(0, CHUNK)], lead.at[pl.ds(0, CHUNK)])

    def scatter_copy(number):
        rows = pl.ds(number * CHUNK, CHUNK)
        at, level = relay_chip(number)
        return remote(cov.at[0, rows], lead.at[rows], one_sent.at[4], one_got.at[4], device(at, 1, level, number // 8))

    @pl.when(scatter)
    def _():
        own_lead.start()
        for number in range(1, 16):
            scatter_copy(number).start()

    side_panel = remote(cov.at[other], panel.at[core], one_sent.at[0], one_got.at[0], sibling)
    pl.when(home)(side_panel.start)
    send_factors(fac_next, 1, z, 0, False)
    send_factors(fac_off, 1, z + 1, 1, False)

    @pl.when(relay)
    def _():
        rows = chunk_rows(relay_place)
        pl.when(scatter)(own_lead.wait)
        arrived = remote(lead.at[rows], lead.at[rows], one_sent.at[4], one_got.at[4], sibling)
        pl.when(jnp.logical_not(scatter))(arrived.wait_recv)
        for number in range(16):
            copy = remote(lead.at[rows], lead.at[rows], lead_sent, lead_got,
                          device(0, number % 8, number // 8 * 4, core))
            pl.when(jnp.logical_not(scatter & (number == 1)))(copy.start)

    def block_rows(number, start=0):
        return pl.ds(pl.multiple_of(start + number * BLOCK, BLOCK), BLOCK)

    def piece(index):
        return pl.ds(pl.multiple_of(index * PIECE, PIECE), PIECE)

    def half_piece(index, which):
        return pl.ds(pl.multiple_of(index * PIECE + which * HALF, HALF), HALF)

    def row_copy(index, sent, target):
        rows = piece(index)
        return remote(buf.at[core, rows], buf.at[core, rows], sent, row_got.at[index], target)

    def side_copy(index, slot):
        rows = piece(index)
        return remote(buf.at[slot, rows], buf.at[slot, rows], side_sent.at[slot], side_got.at[slot, index // (NP // 2)],
                      sibling)

    def source_copy(index, slot, place_to, sent, target):
        rows = piece(index)
        return remote(buf.at[slot, rows], buf.at[place_to, rows], sent, up_got.at[index], target)

    def ring_copy(index, which, sent, got, target):
        rows = half_piece(index, which)
        return remote(buf.at[held, rows], buf.at[2, rows], sent, got.at[index], target)

    z_to = device(x, y, z + jnp.where(back, 7, 1), core)
    xp_to, xm_to = device(x + 1, y, z, core), device(x + 3, y, z, core)
    up_to, down_to = device(x, y + 1, z, core), device(x, y + 7, z, core)

    def send_row(index, to_side):
        def start(condition, copy):
            pl.when(condition)(copy.start)

        start(direct_out, source_copy(index, core, 2, direct_sent, direct_to))
        start(cross_out | cross_home, source_copy(index, core, 2, cross_sent, cross_to))
        start(z_child, row_copy(index, z_sent, z_to))
        start(xm_child, row_copy(index, xm_sent, xm_to))
        start(xp_child, row_copy(index, xp_sent, xp_to))
        start(to_side, side_copy(index, core))

    def side_wait(slot, part):
        total(TILE, side_sent.at[slot], side_got.at[slot, part]).wait_recv()

    def make_panel():
        part_rows = jnp.where(first, half, 1 - half) * 256
        tile_row = core * 16 + row
        side_fac, side_rows = [], pl.ds(pl.multiple_of(part_rows, 256), 256)
        for part in range(2):
            side_fac.append(remote(fac.at[part, side_rows], fac.at[part, side_rows],
                                   one_sent.at[1 + part], one_got.at[1 + part], sibling))
        lead_rows = pl.ds(pl.multiple_of(core * 256, 256), 256)
        side_lead = remote(lead.at[lead_rows], lead.at[lead_rows], one_sent.at[3], one_got.at[3], sibling)

        def split_into(at, load):
            def body(number, carry):
                rows = block_rows(number)
                wide[at, rows], narrow[at, rows] = split(load(rows))
                return carry

            lax.fori_loop(0, BLOCKS, body, 0)

        def send_block(number, start):
            def body(index, carry):
                root_send(start + number * GROUP + index)
                return carry

            lax.fori_loop(0, GROUP, body, 0)

        def root_send(index):
            copy = source_copy(index, 0, 0, direct_sent, device(0, y, turn, turn_core))
            pl.when(turn_out)(copy.start)
            send_row(index, True)

        @pl.when(first)
        def _():
            own_factor.wait()
            total(7 * CHUNK, fac_sent, fac_got.at[0]).wait_recv()

        @pl.when(second)
        def _():
            total(8 * CHUNK, fac_sent, fac_got.at[0]).wait_recv()

        side_fac[0].start()
        band_copy.wait()
        row_band = band[tile_row]
        panel_copy.wait()
        side_panel.wait_recv()
        side_fac[0].wait_recv()
        split_into(0, lambda rows: fac[0, rows])
        kept = (tile_row > 0) & (tile_row <= row_band)

        def first_block(number, carry):
            rows = block_rows(number)
            left = split(jnp.where(kept, panel[0, rows], 0.0))
            buf[core, rows] = dot3(left, (wide[0], narrow[0]), False)
            send_block(number, 0)
            return carry

        lax.fori_loop(0, BLOCKS, first_block, 0)

        def turned_block(number, carry):
            rows = block_rows(number)
            made = dot3(split(buf[core, rows]), (wide[0], narrow[0]), True)
            wide[3, rows], narrow[3, rows] = split(made)
            return carry

        lax.fori_loop(0, BLOCKS, turned_block, 0)
        total(8 * CHUNK, fac_sent, fac_got.at[1]).wait_recv()
        side_fac[1].start()
        pl.when(scatter)(total(7 * CHUNK, lead_sent, lead_got).wait_recv)
        pl.when(jnp.logical_not(scatter))(total(8 * CHUNK, lead_sent, lead_got).wait_recv)
        side_lead.start()
        side_fac[1].wait_recv()
        split_into(1, lambda rows: fac[1, rows])
        lead_kept = band[1] >= 1
        side_lead.wait_recv()
        split_into(2, lambda rows: jnp.where(lead_kept, lead[rows], 0.0))
        panel_kept = (tile_row > 0) & (tile_row - 1 <= row_band)

        def second_block(number, carry):
            rows = block_rows(number)
            update = dot3((wide[3, rows], narrow[3, rows]), (wide[2], narrow[2]), True)
            left = split(jnp.where(panel_kept, panel[1, rows], 0.0) - update)
            made = dot3(left, (wide[1], narrow[1]), False)
            buf[core, block_rows(number, TILE)] = jnp.where(tile_row > 1, made, 0.0)
            send_block(number, NP // 2)
            return carry

        lax.fori_loop(0, BLOCKS, second_block, 0)
        for part in range(2):
            side_wait(other, part)
        for s in range(2):
            def body(number, carry):
                rows = block_rows(number)
                out[s, rows] = buf[s, block_rows(number, core * TILE)]
                return carry

            lax.fori_loop(0, BLOCKS, body, 0)
        side_panel.wait_send()
        side_fac[0].wait_send()
        side_fac[1].wait_send()
        side_lead.wait_send()

        @pl.when(scatter)
        def _():
            total(15 * CHUNK, one_sent.at[4], one_got.at[4]).wait_send()

        pl.when(turn_out)(total(2 * TILE, direct_sent, one_got.at[0]).wait_send)

    def make_base():
        noise_copy.wait()
        morton_copy.wait()
        cov_copy.wait()
        band_copy.wait()
        diagonal = row == lax.rem(col, 16)
        for s in range(2):
            tile = s * 16 + row
            kept = (col <= tile) & (tile - col <= band[tile])
            on_diagonal = diagonal & (col // 16 == s)

            @pl.when(on_diagonal)
            def _():
                turned_noise = noise[...].T
                top = turned_noise.astype(BF16)
                rest = turned_noise - top.astype(F32)
                middle = rest.astype(BF16)
                bottom = (rest - middle.astype(F32)).astype(BF16)
                lanes = lax.broadcasted_iota(jnp.int32, (128, 128), 0)
                for number in range(BLOCKS):
                    stations = morton[pl.ds(tile * BLOCKS + number, 1), :]
                    upper, lower = stations // 128, stations % 128
                    pick = jnp.where(lanes == upper, 1.0, 0.0).astype(BF16)
                    found = jnp.dot(top, pick, preferred_element_type=F32)
                    found = found + (jnp.dot(middle, pick, preferred_element_type=F32)
                                     + jnp.dot(bottom, pick, preferred_element_type=F32))
                    nugget = jnp.sum(jnp.where(lanes == lower, found, 0.0), axis=0, keepdims=True)
                    at = number * BLOCK
                    rows_at = lax.broadcasted_iota(jnp.int32, (BLOCK, TILE), 0) + at
                    cols_at = lax.broadcasted_iota(jnp.int32, (BLOCK, TILE), 1)
                    value = jnp.where(cols_at <= rows_at, out[s, pl.ds(at, BLOCK), :], out[s, :, pl.ds(at, BLOCK)].T)
                    out[s, pl.ds(at, BLOCK), :] = value
                    corner = out[s, pl.ds(at, BLOCK), pl.ds(at, BLOCK)]
                    eye = lanes == lax.broadcasted_iota(jnp.int32, (128, 128), 1)
                    out[s, pl.ds(at, BLOCK), pl.ds(at, BLOCK)] = corner + jnp.where(eye, nugget, 0.0)

            @pl.when(jnp.logical_not(on_diagonal))
            def _():
                def body(number, carry):
                    rows = block_rows(number)
                    out[s, rows] = jnp.where(kept, out[s, rows], 0.0)
                    return carry

                lax.fori_loop(0, BLOCKS, body, 0)

    needed = [away & (col <= s * 16 + row) & (s * 16 + row <= 25) for s in range(2)]
    by_side = [
        away & either(second & either(high & (x == 0), low & (x == 0) & (zl >= 1) & (zl < turn), high & (x == 1) & (zl <= turn),
                                      low & (x == 0) & (zl == turn) & (turn_core == 0)),
                      first & low & (x == 0) & (zl == turn) & (turn_core == 1)),
        away & first & either(low & (x <= 2), tail & either(x <= 2, zl == 0)),
    ]

    def update_block(number):
        part, block = number // BLOCKS, number % BLOCKS

        @pl.when(block == 0)
        def _():
            for s in range(2):
                @pl.when(by_side[s])
                def _():
                    side_wait(s, part)

                @pl.when(needed[s])
                def _():
                    def body(index, carry):
                        rows = block_rows(index)
                        wide[s, rows], narrow[s, rows] = split(buf[s, block_rows(index, part * TILE)])
                        return carry

                    lax.fori_loop(0, BLOCKS, body, 0)

        right = split(buf[held, block_rows(number)])
        columns = pl.ds(pl.multiple_of(block * BLOCK, BLOCK), BLOCK)
        for s in range(2):
            @pl.when(needed[s])
            def _():
                out[s, :, columns] = out[s, :, columns] - dot3((wide[s], narrow[s]), right, True)

    row_delay = depth * ROW_HOP
    col_delay = lag * ROW_HOP
    last_delay = 3 * ROW_HOP
    arrival = jnp.where(ring, col_delay + COL_HOP * jnp.where(here, 0, jnp.maximum(place, 8 - place)), last_delay)
    uses = by_side[0] | turning | (first & row_in), by_side[1] | (second & row_in)
    rows_from = ROW_HOP * jnp.maximum(jnp.where(uses[0], depths[0], 0), jnp.where(uses[1], depths[1], 0))
    update_delay = jnp.maximum(arrival, rows_from + NP // 2 - GROUP + 1)

    def inside(index):
        return (index >= 0) & (index < NP)

    def step(time, carry):
        index = time - row_delay

        @pl.when(row_in & inside(index))
        def _():
            row_copy(index, z_sent, z_to).wait_recv()
            send_row(index, side_out)

        ahead = time - col_delay

        @pl.when(source & inside(ahead))
        def _():
            pl.when(jnp.logical_not(own_row))(source_copy(ahead, 2, 2, up_sent, up_to).wait_recv)

            ring_copy(ahead, 0, up_sent, up_got, up_to).start()
            ring_copy(ahead, 1, down_sent, down_got, down_to).start()

            pl.when(jump_out)(source_copy(ahead, 2, 2, cross_sent, device(2, y, 4, core)).start)

            @pl.when(turning)
            def _():
                side_copy(ahead, 0).start()

                @pl.when(zl >= 2)
                def _():
                    rows = piece(ahead)
                    remote(buf.at[0, rows], buf.at[0, rows], direct_sent, row_got.at[ahead], device(0, y, z + 7, 0)).start()

        going_up = ahead - COL_HOP * place
        going_down = ahead - COL_HOP * (8 - place)
        straight = time - last_delay

        @pl.when(last_in & inside(straight))
        def _():
            source_copy(straight, 2, 2, up_sent, up_to).wait_recv()

        @pl.when(follower & inside(going_up))
        def _():
            copy = ring_copy(going_up, 0, up_sent, up_got, up_to)
            copy.wait_recv()
            pl.when(place <= 6)(copy.start)

        @pl.when(follower & inside(going_down))
        def _():
            copy = ring_copy(going_down, 1, down_sent, down_got, down_to)
            copy.wait_recv()
            pl.when(place >= 2)(copy.start)

        done = time - update_delay + 1

        @pl.when((done > 0) & (done % GROUP == 0) & (done <= NP))
        def _():
            update_block(done // GROUP - 1)

        return carry

    def drain(condition, rows, sent):
        pl.when(condition)(total(rows, sent, one_got.at[0]).wait_send)

    pl.when(home)(make_panel)

    @pl.when(away)
    def _():
        make_base()
        lax.fori_loop(0, update_delay + NP, step, 0)

    drain(z_child, 2 * TILE, z_sent)
    drain(xp_child, 2 * TILE, xp_sent)
    drain(xm_child, 2 * TILE, xm_sent)
    drain(cross_out | cross_home | jump_out, 2 * TILE, cross_sent)
    drain(direct_out | (turning & (zl >= 2)), 2 * TILE, direct_sent)
    drain(send_up, TILE, up_sent)
    drain(send_down, TILE, down_sent)
    for s in range(2):
        drain(either((home | side_out) & (core == s), turning & (s == 0)), 2 * TILE, side_sent.at[s])
    drain(fac_own, 7 * CHUNK, fac_sent)
    drain(fac_far | fac_next | fac_off, 8 * CHUNK, fac_sent)
    drain(relay & scatter, 15 * CHUNK, lead_sent)
    drain(relay & jnp.logical_not(scatter), 16 * CHUNK, lead_sent)


def on_device(cov_tiles, inverse_factors, band, station_noise, morton):
    vmem = pl.BlockSpec(memory_space=pltpu.VMEM)
    hbm = pl.BlockSpec(memory_space=pltpu.HBM)
    dma = pltpu.SemaphoreType.DMA
    out = pl.pallas_call(
        kernel,
        out_shape=jax.ShapeDtypeStruct((2, TILE, TILE), F32),
        in_specs=[hbm] * 5,
        out_specs=vmem,
        scratch_shapes=[
            pltpu.VMEM((3, 2 * TILE, TILE), F32),
            pltpu.VMEM((2, TILE, TILE), F32),
            pltpu.VMEM((2, TILE, TILE), F32),
            pltpu.VMEM((TILE, TILE), F32),
            pltpu.VMEM((4, TILE, TILE), BF16),
            pltpu.VMEM((4, TILE, TILE), BF16),
            pltpu.SMEM((32,), jnp.int32),
            pltpu.VMEM((128, 128), F32),
            pltpu.VMEM((128, 128), jnp.int32),
            dma((NP,)), dma((NP,)), dma((NP,)), dma((2, 2)), dma((2,)), dma, dma((5,)),
            dma, dma, dma, dma, dma, dma, dma, dma((2,)), dma, dma, dma((5,)),
            dma((7,)),
        ],
        compiler_params=pltpu.CompilerParams(
            collective_id=0, has_side_effects=True, vmem_limit_bytes=40 * 1024 * 1024
        ),
        cost_estimate=pl.CostEstimate(flops=6 * 4 * 2 * TILE**3, bytes_accessed=4 * 1024 * 1024, transcendentals=0),
        name="panel_steps",
    )(
        cov_tiles.reshape(2, TILE, TILE),
        inverse_factors,
        band,
        station_noise.reshape(128, 128),
        morton.reshape(128, 128),
    )
    return out.reshape(cov_tiles.shape)


def solution(mesh):
    placed = (P(None, "row", None, "col", None, None), P(None, "row", None), P(), P(), P())
    return jax.shard_map(
        on_device,
        mesh=mesh,
        in_specs=placed,
        out_specs=P(None, "row", None, "col", None, None),
        check_vma=False,
    )
```

```python
import jax
import jax.numpy as jnp
from jax import lax
from jax.experimental import pallas as pl
from jax.experimental.pallas import tpu as pltpu
from jax.sharding import PartitionSpec as P

TILE = 512
BLOCK = 128
BLOCKS = TILE // BLOCK
NP = 32
PIECE = 2 * TILE // NP
HALF = PIECE // 2
GROUP = BLOCK // PIECE
ROW_HOP = 4
COL_HOP = 5
TIP = 4
BULK = NP - TIP
SLACK = 8
CHUNK = TILE // 16
MESH = pl.DeviceIdType.MESH
F32 = jnp.float32
BF16 = jnp.bfloat16


def device(x, y, z, core):
    x, y, z = lax.rem(x + 4, 4), lax.rem(y + 8, 8), lax.rem(z + 8, 8)
    return (z // 4 * 8 + y, x * 8 + z % 4 * 2 + core)


def split(value):
    high = value.astype(BF16)
    return high, (value - high.astype(F32)).astype(BF16)


def dot3(a, b, transposed):
    dims = (((1,), (1 if transposed else 0,)), ((), ()))

    def dot(p, q):
        return lax.dot_general(p, q, dims, preferred_element_type=F32)

    return dot(a[0], b[0]) + (dot(a[0], b[1]) + dot(a[1], b[0]))


def either(*conditions):
    result = conditions[0]
    for condition in conditions[1:]:
        result = result | condition
    return result


def count(*conditions):
    return sum(jnp.where(condition, 1, 0) for condition in conditions)


def kernel(cov, factors, band_in, noise_in, morton_in, out, buf, panel, fac, lead, wide, narrow, band, noise, morton,
           row_got, up_got, down_got, side_got, fac_got, lead_got, one_got,
           z_sent, xp_sent, xm_sent, cross_sent, direct_sent, up_sent, down_sent, side_sent, fac_sent, lead_sent, one_sent,
           tip_sent, local):
    row = lax.axis_index("row")
    col = lax.axis_index("col")
    half, y = row // 8, row % 8
    x, zl, core = col // 8, col % 8 // 2, col % 2
    z = half * 4 + zl
    other = 1 - core
    sibling = device(x, y, z, other)
    home = (x == 0) & (zl == 0)
    away = jnp.logical_not(home)
    first, second = core == 0, core == 1
    low, high = half == 0, half == 1
    tail = high & (y <= 1)
    turn, turn_core = y // 2, y % 2

    back = first & low & (x == 0) & (zl >= 1) & (zl < turn)
    from_below = (zl >= 1) & either(first & high & (x == 0), second & low & (x == 1), second & tail & (x == 2))
    from_xm = either(first & high & (x == 1) & (zl <= turn), second & low & either(x == 2, (x == 1) & (zl == 0)))
    from_xp = either(second & low & (x == 0) & (zl >= 1), second & low & (x == 3) & (zl == 0),
                     second & tail & either((x == 3) & (zl == 0), (x == 2) & (zl == 0), x == 1, (x == 0) & (zl >= 1)))
    row_in = either(back, from_below, from_xm, from_xp)
    z_child = either((zl < 3) & either(first & high & (x == 0), second & low & (x == 1), second & tail & (x == 2)),
                     back & (zl >= 2))
    xp_child = either(first & high & (x == 0) & (zl <= turn), second & low & either(x == 1, home))
    xm_child = either(second & low & either((x == 1) & (zl >= 1), home),
                      second & tail & either(home, (x == 3) & (zl == 0), x == 2, (x == 1) & (zl >= 1)))
    side_out = row_in & jnp.logical_not((x == 3) & low)
    depth_low = jnp.where((x == 1) | (x == 3), zl + 1, zl + 2)
    depth_tail = jnp.where(x == 3, 1, zl + jnp.where(x == 2, 2, jnp.where(x == 1, 3, 4)))
    depths = jnp.where(low, turn - zl + 1, zl + x), jnp.where(low, depth_low, depth_tail)
    depth = jnp.where(first, depths[0], depths[1])

    place = lax.rem(y - 2 * zl - core + 8, 8)
    here = place == 0
    ring = away & (x <= 2)
    source = ring & here
    follower = ring & jnp.logical_not(here)
    turning = source & (x == 0) & low
    own_row = (x == 1) & high & (zl == 0) & (y == 0) & first
    last_out = (x == 3) & (zl == 0) & high & (y == 0) & second
    last_in = (x == 3) & (zl == 0) & high & (y == 1) & first
    last_own = (x == 3) & (zl == 0) & tail & jnp.logical_not(last_in)
    lag = jnp.where(x == 0, 1, jnp.where((x == 1) & low, jnp.where(zl == 0, 2, 1),
                                          jnp.where((x == 2) & high & (zl == 0), 3, 2)))
    held = jnp.where(turning | own_row, 0, jnp.where(last_own, 1, 2))
    send_up = ring & (place <= 6)
    send_down = ring & (place != 1)
    tip_up = ring & (place <= 3)
    tip_down = ring & (here | (place >= 6))

    turn_out = home & first & low & (y >= 2)
    cross_home = home & first & (y >= 2)
    cross_near = (x == 1) & (zl == 0) & tail & first
    feed_row = (x == 1) & (zl == 0) & high & first & (y >= 1)
    feed_far = (x == 3) & (zl == 0) & low & second
    direct_out = feed_row | feed_far | last_out
    cross_out = cross_near | (feed_far & (y >= 2))
    jump_out = source & (x == 2) & low & (zl == 0)
    direct_x = jnp.where(last_out, 3, jnp.where(feed_far, 2, 1))
    direct_to = device(direct_x, jnp.where(last_out, 1, y), half * 4 + jnp.where(last_out, 0, turn),
                       jnp.where(last_out, 0, turn_core))
    cross_to = device(jnp.where(feed_far, 2, half), y, (1 - half) * 4 + turn, turn_core)

    fac_own = home & second
    fac_far = (x == 0) & (zl == 3) & second
    fac_next = (x == 1) & (zl == 0) & first
    fac_off = (x == 3) & (zl == 3) & second
    scatter = home & low & (y == 1) & first
    relay = (y == 1) & either(first & ((z == 7) | (z == 2)), second & ((z == 1) | (z == 6)))
    relay_place = core * 8 + x + jnp.where((z == 7) | (z == 1), 0, 4)

    def relay_chip(number):
        return number % 4, (7, 2, 1, 6)[number // 4]

    def local_copy(number, src, dst):
        return pltpu.make_async_copy(src, dst, local.at[number])

    band_copy = local_copy(0, band_in, band)
    noise_copy = local_copy(1, noise_in, noise)
    morton_copy = local_copy(2, morton_in, morton)
    cov_copy = local_copy(3, cov, out)
    panel_copy = local_copy(4, cov.at[core], panel.at[core])
    band_copy.start()

    @pl.when(home)
    def _():
        panel_copy.start()

    @pl.when(away)
    def _():
        noise_copy.start()
        morton_copy.start()
        cov_copy.start()

    barrier = pltpu.get_barrier_semaphore()

    def greet(target):
        pl.semaphore_signal(barrier, inc=1, device_id=target, device_id_type=MESH)

    def greet_if(condition, target):
        @pl.when(condition)
        def _():
            greet(target)

    greet(sibling)

    @pl.when(home)
    def _():
        for step in range(8):
            @pl.when(first)
            def _():
                greet(device(0, step, z, 1))
                greet(device(1, step, z, 0))
                at, level = relay_chip(step)
                greet(device(at, 1, level, 0))

            @pl.when(second)
            def _():
                greet(device(0, step, z + 7, 1))
                greet(device(3, step, z + 7, 1))
                at, level = relay_chip(8 + step)
                greet(device(at, 1, level, 1))

    greet_if(relay, device(0, 1, 0, 0))
    greet_if(back, device(0, y, z + 1, jnp.where(zl + 1 == turn, turn_core, 0)))
    greet_if(from_below, device(x, y, z + 7, core))
    greet_if(from_xm, device(x + 3, y, z, core))
    greet_if(from_xp, device(x + 1, y, z, core))
    greet_if(follower, device(x, y + 7, z, core))
    greet_if(follower, device(x, y + 1, z, core))
    greet_if(turning, device(0, y, 0, 0))
    greet_if(source & (x == 0) & high, device(0, y, 0, 0))
    greet_if(source & (x == 1) & low, device(jnp.where(zl == 0, 1, 0), y, 4, 0))
    greet_if(source & (x == 1) & high & jnp.logical_not(own_row), device(1, y, 4, 0))
    jump_in = source & (x == 2) & high & (zl == 0)
    greet_if(source & (x == 2) & jnp.logical_not(jump_in), device(3, y, 0, 1))
    greet_if(jump_in, device(2, y, 0, core))
    greet_if(last_in, device(3, 0, 4, 1))
    targets = 1 + count(z_child, xp_child, xm_child, send_up, send_down, turn_out, cross_home, direct_out, cross_out, jump_out,
                        turning & (zl >= 2))
    targets = targets + 8 * count(fac_own, fac_far, fac_next, fac_off) + 16 * count(relay, scatter)
    pl.semaphore_wait(barrier, targets)

    def remote(src, dst, sent, got, target):
        return pltpu.make_async_remote_copy(
            src_ref=src, dst_ref=dst, send_sem=sent, recv_sem=got, device_id=target, device_id_type=MESH
        )

    def total(rows, sent, got):
        return remote(buf.at[0, pl.ds(0, rows)], buf.at[0, pl.ds(0, rows)], sent, got, sibling)

    def chunk_rows(number):
        return pl.ds(pl.multiple_of(number * CHUNK, CHUNK), CHUNK)

    def send_factors(condition, part, which, target_z, target_core):
        rows = pl.ds(which * (CHUNK // 2), CHUNK // 2)
        there = pl.ds(pl.multiple_of(row * CHUNK + which * (CHUNK // 2), CHUNK // 2), CHUNK // 2)

        @pl.when(condition)
        def _():
            for step in range(8):
                remote(factors.at[part, rows], fac.at[part, there], fac_sent, fac_got.at[part],
                       device(0, step, target_z, target_core)).start()

    def send_part(part):
        send_factors(fac_own, part, 0, z, 0)
        send_factors(fac_next, part, 1, z, 0)
        send_factors(fac_far, part, 0, z + 1, 1)
        send_factors(fac_off, part, 1, z + 1, 1)

    send_part(0)

    def scatter_copy(number):
        rows = pl.ds(number * CHUNK, CHUNK)
        at, level = relay_chip(number)
        return remote(cov.at[0, rows], lead.at[rows], one_sent.at[4], one_got.at[4], device(at, 1, level, number // 8))

    @pl.when(scatter)
    def _():
        for number in range(16):
            scatter_copy(number).start()

    side_panel = remote(cov.at[other], panel.at[core], one_sent.at[0], one_got.at[0], sibling)
    pl.when(home)(side_panel.start)
    send_part(1)

    @pl.when(relay)
    def _():
        rows = chunk_rows(relay_place)
        remote(lead.at[rows], lead.at[rows], one_sent.at[4], one_got.at[4], sibling).wait_recv()
        for number in range(16):
            remote(lead.at[rows], lead.at[rows], lead_sent, lead_got,
                   device(0, number % 8, number // 8 * 4, core)).start()

    def block_rows(number, start=0):
        return pl.ds(pl.multiple_of(start + number * BLOCK, BLOCK), BLOCK)

    def piece(index):
        return pl.ds(pl.multiple_of(index * PIECE, PIECE), PIECE)

    def half_piece(index, which):
        return pl.ds(pl.multiple_of(index * PIECE + which * HALF, HALF), HALF)

    def row_copy(index, sent, target):
        rows = piece(index)
        return remote(buf.at[core, rows], buf.at[core, rows], sent, row_got.at[index], target)

    def side_copy(index, slot):
        rows = piece(index)
        return remote(buf.at[slot, rows], buf.at[slot, rows], side_sent.at[slot], side_got.at[slot, index // (NP // 2)],
                      sibling)

    def source_copy(index, slot, place_to, sent, target):
        rows = piece(index)
        return remote(buf.at[slot, rows], buf.at[place_to, rows], sent, up_got.at[index], target)

    def tip_copy(index, which, got, target):
        rows = piece(index)
        return remote(buf.at[held, rows], buf.at[2, rows], tip_sent.at[which], got.at[index], target)

    def ring_copy(index, which, sent, got, target):
        rows = half_piece(index, which)
        return remote(buf.at[held, rows], buf.at[2, rows], sent, got.at[index], target)

    z_to = device(x, y, z + jnp.where(back, 7, 1), core)
    xp_to, xm_to = device(x + 1, y, z, core), device(x + 3, y, z, core)
    up_to, down_to = device(x, y + 1, z, core), device(x, y + 7, z, core)

    def send_row(index, to_side):
        def start(condition, copy):
            pl.when(condition)(copy.start)

        start(direct_out, source_copy(index, core, 2, direct_sent, direct_to))
        start(cross_out | cross_home, source_copy(index, core, 2, cross_sent, cross_to))
        start(z_child, row_copy(index, z_sent, z_to))
        start(xm_child, row_copy(index, xm_sent, xm_to))
        start(xp_child, row_copy(index, xp_sent, xp_to))
        start(to_side, side_copy(index, core))

    def side_wait(slot, part):
        total(TILE, side_sent.at[slot], side_got.at[slot, part]).wait_recv()

    def make_panel():
        part_rows = jnp.where(first, half, 1 - half) * 256
        tile_row = core * 16 + row
        side_fac, side_rows = [], pl.ds(pl.multiple_of(part_rows, 256), 256)
        for part in range(2):
            side_fac.append(remote(fac.at[part, side_rows], fac.at[part, side_rows],
                                   one_sent.at[1 + part], one_got.at[1 + part], sibling))
        lead_rows = pl.ds(pl.multiple_of(core * 256, 256), 256)
        side_lead = remote(lead.at[lead_rows], lead.at[lead_rows], one_sent.at[3], one_got.at[3], sibling)

        def split_into(at, load):
            def body(number, carry):
                rows = block_rows(number)
                wide[at, rows], narrow[at, rows] = split(load(rows))
                return carry

            lax.fori_loop(0, BLOCKS, body, 0)

        def send_block(number, start):
            def body(index, carry):
                root_send(start + number * GROUP + index)
                return carry

            lax.fori_loop(0, GROUP, body, 0)

        def root_send(index):
            copy = source_copy(index, 0, 0, direct_sent, device(0, y, turn, turn_core))
            pl.when(turn_out)(copy.start)
            send_row(index, True)

        total(8 * CHUNK, fac_sent, fac_got.at[0]).wait_recv()
        side_fac[0].start()
        band_copy.wait()
        row_band = band[tile_row]
        panel_copy.wait()
        side_panel.wait_recv()
        side_fac[0].wait_recv()
        split_into(0, lambda rows: fac[0, rows])
        kept = (tile_row > 0) & (tile_row <= row_band)

        def first_block(number, carry):
            rows = block_rows(number)
            left = split(jnp.where(kept, panel[0, rows], 0.0))
            buf[core, rows] = dot3(left, (wide[0], narrow[0]), False)
            send_block(number, 0)
            return carry

        lax.fori_loop(0, BLOCKS, first_block, 0)

        def turned_block(number, carry):
            rows = block_rows(number)
            made = dot3(split(buf[core, rows]), (wide[0], narrow[0]), True)
            wide[3, rows], narrow[3, rows] = split(made)
            return carry

        lax.fori_loop(0, BLOCKS, turned_block, 0)
        total(8 * CHUNK, fac_sent, fac_got.at[1]).wait_recv()
        side_fac[1].start()
        total(8 * CHUNK, lead_sent, lead_got).wait_recv()
        side_lead.start()
        side_fac[1].wait_recv()
        split_into(1, lambda rows: fac[1, rows])
        lead_kept = band[1] >= 1
        side_lead.wait_recv()
        split_into(2, lambda rows: jnp.where(lead_kept, lead[rows], 0.0))
        panel_kept = (tile_row > 0) & (tile_row - 1 <= row_band)

        def second_block(number, carry):
            rows = block_rows(number)
            update = dot3((wide[3, rows], narrow[3, rows]), (wide[2], narrow[2]), True)
            left = split(jnp.where(panel_kept, panel[1, rows], 0.0) - update)
            made = dot3(left, (wide[1], narrow[1]), False)
            buf[core, block_rows(number, TILE)] = jnp.where(tile_row > 1, made, 0.0)
            send_block(number, NP // 2)
            return carry

        lax.fori_loop(0, BLOCKS, second_block, 0)
        for part in range(2):
            side_wait(other, part)
        for s in range(2):
            def body(number, carry):
                rows = block_rows(number)
                out[s, rows] = buf[s, block_rows(number, core * TILE)]
                return carry

            lax.fori_loop(0, BLOCKS, body, 0)
        side_panel.wait_send()
        side_fac[0].wait_send()
        side_fac[1].wait_send()
        side_lead.wait_send()

        @pl.when(scatter)
        def _():
            total(16 * CHUNK, one_sent.at[4], one_got.at[4]).wait_send()

        pl.when(turn_out)(total(2 * TILE, direct_sent, one_got.at[0]).wait_send)

    def make_base():
        noise_copy.wait()
        morton_copy.wait()
        cov_copy.wait()
        band_copy.wait()
        diagonal = row == lax.rem(col, 16)
        for s in range(2):
            tile = s * 16 + row
            kept = (col <= tile) & (tile - col <= band[tile])
            on_diagonal = diagonal & (col // 16 == s)

            @pl.when(on_diagonal)
            def _():
                turned_noise = noise[...].T
                top = turned_noise.astype(BF16)
                rest = turned_noise - top.astype(F32)
                middle = rest.astype(BF16)
                bottom = (rest - middle.astype(F32)).astype(BF16)
                lanes = lax.broadcasted_iota(jnp.int32, (128, 128), 0)
                for number in range(BLOCKS):
                    stations = morton[pl.ds(tile * BLOCKS + number, 1), :]
                    upper, lower = stations // 128, stations % 128
                    pick = jnp.where(lanes == upper, 1.0, 0.0).astype(BF16)
                    found = jnp.dot(top, pick, preferred_element_type=F32)
                    found = found + (jnp.dot(middle, pick, preferred_element_type=F32)
                                     + jnp.dot(bottom, pick, preferred_element_type=F32))
                    nugget = jnp.sum(jnp.where(lanes == lower, found, 0.0), axis=0, keepdims=True)
                    at = number * BLOCK
                    rows_at = lax.broadcasted_iota(jnp.int32, (BLOCK, TILE), 0) + at
                    cols_at = lax.broadcasted_iota(jnp.int32, (BLOCK, TILE), 1)
                    value = jnp.where(cols_at <= rows_at, out[s, pl.ds(at, BLOCK), :], out[s, :, pl.ds(at, BLOCK)].T)
                    out[s, pl.ds(at, BLOCK), :] = value
                    corner = out[s, pl.ds(at, BLOCK), pl.ds(at, BLOCK)]
                    eye = lanes == lax.broadcasted_iota(jnp.int32, (128, 128), 1)
                    out[s, pl.ds(at, BLOCK), pl.ds(at, BLOCK)] = corner + jnp.where(eye, nugget, 0.0)

            @pl.when(jnp.logical_not(on_diagonal))
            def _():
                def body(number, carry):
                    rows = block_rows(number)
                    out[s, rows] = jnp.where(kept, out[s, rows], 0.0)
                    return carry

                lax.fori_loop(0, BLOCKS, body, 0)

    needed = [away & (col <= s * 16 + row) & (s * 16 + row <= 25) for s in range(2)]
    by_side = [
        away & either(second & either(high & (x == 0), low & (x == 0) & (zl >= 1) & (zl < turn), high & (x == 1) & (zl <= turn),
                                      low & (x == 0) & (zl == turn) & (turn_core == 0)),
                      first & low & (x == 0) & (zl == turn) & (turn_core == 1)),
        away & first & either(low & (x <= 2), tail & either(x <= 2, zl == 0)),
    ]

    def update_block(number):
        part, block = number // BLOCKS, number % BLOCKS

        @pl.when(block == 0)
        def _():
            for s in range(2):
                @pl.when(by_side[s])
                def _():
                    side_wait(s, part)

                @pl.when(needed[s])
                def _():
                    def body(index, carry):
                        rows = block_rows(index)
                        wide[s, rows], narrow[s, rows] = split(buf[s, block_rows(index, part * TILE)])
                        return carry

                    lax.fori_loop(0, BLOCKS, body, 0)

        right = split(buf[held, block_rows(number)])
        columns = pl.ds(pl.multiple_of(block * BLOCK, BLOCK), BLOCK)
        for s in range(2):
            @pl.when(needed[s])
            def _():
                out[s, :, columns] = out[s, :, columns] - dot3((wide[s], narrow[s]), right, True)

    row_delay = depth * ROW_HOP
    col_delay = lag * ROW_HOP
    last_delay = 3 * ROW_HOP
    arrival = jnp.where(ring, col_delay + COL_HOP * jnp.where(here, 0, jnp.maximum(place, 8 - place)), last_delay)
    uses = by_side[0] | turning | (first & row_in), by_side[1] | (second & row_in)
    rows_from = ROW_HOP * jnp.maximum(jnp.where(uses[0], depths[0], 0), jnp.where(uses[1], depths[1], 0))
    update_delay = jnp.maximum(arrival, rows_from + SLACK + NP // 2 - GROUP + 1)

    def inside(index):
        return (index >= 0) & (index < NP)

    def in_bulk(index):
        return (index >= 0) & (index < BULK)

    def step(time, carry):
        index = time - row_delay

        @pl.when(row_in & inside(index))
        def _():
            row_copy(index, z_sent, z_to).wait_recv()
            send_row(index, side_out)

        ahead = time - col_delay

        @pl.when(source & inside(ahead))
        def _():
            pl.when(jnp.logical_not(own_row))(source_copy(ahead, 2, 2, up_sent, up_to).wait_recv)

            @pl.when(ahead < BULK)
            def _():
                ring_copy(ahead, 0, up_sent, up_got, up_to).start()
                ring_copy(ahead, 1, down_sent, down_got, down_to).start()

            @pl.when(ahead >= BULK)
            def _():
                tip_copy(ahead, 0, up_got, up_to).start()
                tip_copy(ahead, 1, down_got, down_to).start()

            pl.when(jump_out)(source_copy(ahead, 2, 2, cross_sent, device(2, y, 4, core)).start)

            @pl.when(turning)
            def _():
                side_copy(ahead, 0).start()

                @pl.when(zl >= 2)
                def _():
                    rows = piece(ahead)
                    remote(buf.at[0, rows], buf.at[0, rows], direct_sent, row_got.at[ahead], device(0, y, z + 7, 0)).start()

        going_up = ahead - COL_HOP * place
        going_down = ahead - COL_HOP * (8 - place)
        straight = time - last_delay

        @pl.when(last_in & inside(straight))
        def _():
            source_copy(straight, 2, 2, up_sent, up_to).wait_recv()

        @pl.when(follower & (place <= 4) & (going_up >= BULK) & (going_up < NP))
        def _():
            copy = tip_copy(going_up, 0, up_got, up_to)
            copy.wait_recv()
            pl.when(place <= 3)(copy.start)

        @pl.when(follower & (place >= 5) & (going_down >= BULK) & (going_down < NP))
        def _():
            copy = tip_copy(going_down, 1, down_got, down_to)
            copy.wait_recv()
            pl.when(place >= 6)(copy.start)

        @pl.when(follower & in_bulk(going_up))
        def _():
            copy = ring_copy(going_up, 0, up_sent, up_got, up_to)
            copy.wait_recv()
            pl.when(place <= 6)(copy.start)

        @pl.when(follower & in_bulk(going_down))
        def _():
            copy = ring_copy(going_down, 1, down_sent, down_got, down_to)
            copy.wait_recv()
            pl.when(place >= 2)(copy.start)

        done = time - update_delay + 1

        @pl.when((done > 0) & (done % GROUP == 0) & (done <= NP))
        def _():
            update_block(done // GROUP - 1)

        return carry

    def drain(condition, rows, sent):
        pl.when(condition)(total(rows, sent, one_got.at[0]).wait_send)

    pl.when(home)(make_panel)

    @pl.when(away)
    def _():
        make_base()
        lax.fori_loop(0, update_delay + NP, step, 0)

    drain(z_child, 2 * TILE, z_sent)
    drain(xp_child, 2 * TILE, xp_sent)
    drain(xm_child, 2 * TILE, xm_sent)
    drain(cross_out | cross_home | jump_out, 2 * TILE, cross_sent)
    drain(direct_out | (turning & (zl >= 2)), 2 * TILE, direct_sent)
    drain(send_up, BULK * HALF, up_sent)
    drain(send_down, BULK * HALF, down_sent)
    drain(tip_up, TIP * PIECE, tip_sent.at[0])
    drain(tip_down, TIP * PIECE, tip_sent.at[1])
    for s in range(2):
        drain(either((home | side_out) & (core == s), turning & (s == 0)), 2 * TILE, side_sent.at[s])
    drain(either(fac_own, fac_far, fac_next, fac_off), 8 * CHUNK, fac_sent)
    drain(relay, 16 * CHUNK, lead_sent)


def on_device(cov_tiles, inverse_factors, band, station_noise, morton):
    vmem = pl.BlockSpec(memory_space=pltpu.VMEM)
    hbm = pl.BlockSpec(memory_space=pltpu.HBM)
    dma = pltpu.SemaphoreType.DMA
    out = pl.pallas_call(
        kernel,
        out_shape=jax.ShapeDtypeStruct((2, TILE, TILE), F32),
        in_specs=[hbm] * 5,
        out_specs=vmem,
        scratch_shapes=[
            pltpu.VMEM((3, 2 * TILE, TILE), F32),
            pltpu.VMEM((2, TILE, TILE), F32),
            pltpu.VMEM((2, TILE, TILE), F32),
            pltpu.VMEM((TILE, TILE), F32),
            pltpu.VMEM((4, TILE, TILE), BF16),
            pltpu.VMEM((4, TILE, TILE), BF16),
            pltpu.SMEM((32,), jnp.int32),
            pltpu.VMEM((128, 128), F32),
            pltpu.VMEM((128, 128), jnp.int32),
            dma((NP,)), dma((NP,)), dma((NP,)), dma((2, 2)), dma((2,)), dma, dma((5,)),
            dma, dma, dma, dma, dma, dma, dma, dma((2,)), dma, dma, dma((5,)),
            dma((2,)), dma((5,)),
        ],
        compiler_params=pltpu.CompilerParams(
            collective_id=0, has_side_effects=True, vmem_limit_bytes=40 * 1024 * 1024
        ),
        cost_estimate=pl.CostEstimate(flops=6 * 4 * 2 * TILE**3, bytes_accessed=4 * 1024 * 1024, transcendentals=0),
        name="panel_steps",
    )(
        *(
            pltpu.with_memory_space_constraint(operand, pltpu.HBM)
            for operand in (
                cov_tiles.reshape(2, TILE, TILE),
                inverse_factors,
                band,
                station_noise.reshape(128, 128),
                morton.reshape(128, 128),
            )
        )
    )
    return out.reshape(cov_tiles.shape)


def solution(mesh):
    placed = (P(None, "row", None, "col", None, None), P(None, "row", None), P(), P(), P())
    return jax.shard_map(
        on_device,
        mesh=mesh,
        in_specs=placed,
        out_specs=P(None, "row", None, "col", None, None),
        check_vma=False,
    )
```

```python
import jax
import jax.numpy as jnp
from jax import lax
from jax.experimental import pallas as pl
from jax.experimental.pallas import tpu as pltpu
from jax.sharding import PartitionSpec as P

TILE = 512
BLOCK = 128
BLOCKS = TILE // BLOCK
NP = 64
PIECE = 2 * TILE // NP
HALF = PIECE // 2
GROUP = BLOCK // PIECE
ROW_HOP = 8
COL_HOP = 10
TIP = 8
BULK = NP - TIP
SLACK = 16
CHUNK = TILE // 16
MESH = pl.DeviceIdType.MESH
F32 = jnp.float32
BF16 = jnp.bfloat16


def device(x, y, z, core):
    x, y, z = lax.rem(x + 4, 4), lax.rem(y + 8, 8), lax.rem(z + 8, 8)
    return (z // 4 * 8 + y, x * 8 + z % 4 * 2 + core)


def split(value):
    high = value.astype(BF16)
    return high, (value - high.astype(F32)).astype(BF16)


def dot3(a, b, transposed):
    dims = (((1,), (1 if transposed else 0,)), ((), ()))

    def dot(p, q):
        return lax.dot_general(p, q, dims, preferred_element_type=F32)

    return dot(a[0], b[0]) + (dot(a[0], b[1]) + dot(a[1], b[0]))


def either(*conditions):
    result = conditions[0]
    for condition in conditions[1:]:
        result = result | condition
    return result


def count(*conditions):
    return sum(jnp.where(condition, 1, 0) for condition in conditions)


def kernel(cov, factors, band_in, noise_in, morton_in, out, buf, panel, fac, lead, wide, narrow, band, noise, morton,
           row_got, up_got, down_got, side_got, fac_got, lead_got, one_got,
           z_sent, xp_sent, xm_sent, cross_sent, direct_sent, up_sent, down_sent, side_sent, fac_sent, lead_sent, one_sent,
           tip_sent, local):
    row = lax.axis_index("row")
    col = lax.axis_index("col")
    half, y = row // 8, row % 8
    x, zl, core = col // 8, col % 8 // 2, col % 2
    z = half * 4 + zl
    other = 1 - core
    sibling = device(x, y, z, other)
    home = (x == 0) & (zl == 0)
    away = jnp.logical_not(home)
    first, second = core == 0, core == 1
    low, high = half == 0, half == 1
    tail = high & (y <= 1)
    turn, turn_core = y // 2, y % 2

    back = first & low & (x == 0) & (zl >= 1) & (zl < turn)
    from_below = (zl >= 1) & either(first & high & (x == 0), second & low & (x == 1), second & tail & (x == 2))
    from_xm = either(first & high & (x == 1) & (zl <= turn), second & low & either(x == 2, (x == 1) & (zl == 0)))
    from_xp = either(second & low & (x == 0) & (zl >= 1), second & low & (x == 3) & (zl == 0),
                     second & tail & either((x == 3) & (zl == 0), (x == 2) & (zl == 0), x == 1, (x == 0) & (zl >= 1)))
    row_in = either(back, from_below, from_xm, from_xp)
    z_child = either((zl < 3) & either(first & high & (x == 0), second & low & (x == 1), second & tail & (x == 2)),
                     back & (zl >= 2))
    xp_child = either(first & high & (x == 0) & (zl <= turn), second & low & either(x == 1, home))
    xm_child = either(second & low & either((x == 1) & (zl >= 1), home),
                      second & tail & either(home, (x == 3) & (zl == 0), x == 2, (x == 1) & (zl >= 1)))
    side_out = row_in & jnp.logical_not((x == 3) & low)
    depth_low = jnp.where((x == 1) | (x == 3), zl + 1, zl + 2)
    depth_tail = jnp.where(x == 3, 1, zl + jnp.where(x == 2, 2, jnp.where(x == 1, 3, 4)))
    depths = jnp.where(low, turn - zl + 1, zl + x), jnp.where(low, depth_low, depth_tail)
    depth = jnp.where(first, depths[0], depths[1])

    place = lax.rem(y - 2 * zl - core + 8, 8)
    here = place == 0
    ring = away & (x <= 2)
    source = ring & here
    follower = ring & jnp.logical_not(here)
    turning = source & (x == 0) & low
    own_row = (x == 1) & high & (zl == 0) & (y == 0) & first
    last_out = (x == 3) & (zl == 0) & high & (y == 0) & second
    last_in = (x == 3) & (zl == 0) & high & (y == 1) & first
    last_own = (x == 3) & (zl == 0) & tail & jnp.logical_not(last_in)
    lag = jnp.where(x == 0, 1, jnp.where((x == 1) & low, jnp.where(zl == 0, 2, 1),
                                          jnp.where((x == 2) & high & (zl == 0), 3, 2)))
    held = jnp.where(turning | own_row, 0, jnp.where(last_own, 1, 2))
    send_up = ring & (place <= 6)
    send_down = ring & (place != 1)
    tip_up = ring & (place <= 3)
    tip_down = ring & (here | (place >= 6))

    turn_out = home & first & low & (y >= 2)
    cross_home = home & first & (y >= 2)
    cross_near = (x == 1) & (zl == 0) & tail & first
    feed_row = (x == 1) & (zl == 0) & high & first & (y >= 1)
    feed_far = (x == 3) & (zl == 0) & low & second
    direct_out = feed_row | feed_far | last_out
    cross_out = cross_near | (feed_far & (y >= 2))
    jump_out = source & (x == 2) & low & (zl == 0)
    direct_x = jnp.where(last_out, 3, jnp.where(feed_far, 2, 1))
    direct_to = device(direct_x, jnp.where(last_out, 1, y), half * 4 + jnp.where(last_out, 0, turn),
                       jnp.where(last_out, 0, turn_core))
    cross_to = device(jnp.where(feed_far, 2, half), y, (1 - half) * 4 + turn, turn_core)

    fac_own = home & second
    fac_far = (x == 0) & (zl == 3) & second
    fac_next = (x == 1) & (zl == 0) & first
    fac_off = (x == 3) & (zl == 3) & second
    scatter = home & low & (y == 1) & first
    relay = (y == 1) & either(first & ((z == 7) | (z == 2)), second & ((z == 1) | (z == 6)))
    relay_place = core * 8 + x + jnp.where((z == 7) | (z == 1), 0, 4)

    def relay_chip(number):
        return number % 4, (7, 2, 1, 6)[number // 4]

    def local_copy(number, src, dst):
        return pltpu.make_async_copy(src, dst, local.at[number])

    band_copy = local_copy(0, band_in, band)
    noise_copy = local_copy(1, noise_in, noise)
    morton_copy = local_copy(2, morton_in, morton)
    cov_copy = local_copy(3, cov, out)
    panel_copy = local_copy(4, cov.at[core], panel.at[core])
    band_copy.start()

    @pl.when(home)
    def _():
        panel_copy.start()

    @pl.when(away)
    def _():
        noise_copy.start()
        morton_copy.start()
        cov_copy.start()

    barrier = pltpu.get_barrier_semaphore()

    def greet(target):
        pl.semaphore_signal(barrier, inc=1, device_id=target, device_id_type=MESH)

    def greet_if(condition, target):
        @pl.when(condition)
        def _():
            greet(target)

    greet(sibling)

    @pl.when(home)
    def _():
        for step in range(8):
            @pl.when(first)
            def _():
                greet(device(0, step, z, 1))
                greet(device(1, step, z, 0))
                at, level = relay_chip(step)
                greet(device(at, 1, level, 0))

            @pl.when(second)
            def _():
                greet(device(0, step, z + 7, 1))
                greet(device(3, step, z + 7, 1))
                at, level = relay_chip(8 + step)
                greet(device(at, 1, level, 1))

    greet_if(relay, device(0, 1, 0, 0))
    greet_if(back, device(0, y, z + 1, jnp.where(zl + 1 == turn, turn_core, 0)))
    greet_if(from_below, device(x, y, z + 7, core))
    greet_if(from_xm, device(x + 3, y, z, core))
    greet_if(from_xp, device(x + 1, y, z, core))
    greet_if(follower, device(x, y + 7, z, core))
    greet_if(follower, device(x, y + 1, z, core))
    greet_if(turning, device(0, y, 0, 0))
    greet_if(source & (x == 0) & high, device(0, y, 0, 0))
    greet_if(source & (x == 1) & low, device(jnp.where(zl == 0, 1, 0), y, 4, 0))
    greet_if(source & (x == 1) & high & jnp.logical_not(own_row), device(1, y, 4, 0))
    jump_in = source & (x == 2) & high & (zl == 0)
    greet_if(source & (x == 2) & jnp.logical_not(jump_in), device(3, y, 0, 1))
    greet_if(jump_in, device(2, y, 0, core))
    greet_if(last_in, device(3, 0, 4, 1))
    targets = 1 + count(z_child, xp_child, xm_child, send_up, send_down, turn_out, cross_home, direct_out, cross_out, jump_out,
                        turning & (zl >= 2))
    targets = targets + 8 * count(fac_own, fac_far, fac_next, fac_off) + 16 * count(relay, scatter)
    pl.semaphore_wait(barrier, targets)

    def remote(src, dst, sent, got, target):
        return pltpu.make_async_remote_copy(
            src_ref=src, dst_ref=dst, send_sem=sent, recv_sem=got, device_id=target, device_id_type=MESH
        )

    def total(rows, sent, got):
        return remote(buf.at[0, pl.ds(0, rows)], buf.at[0, pl.ds(0, rows)], sent, got, sibling)

    def chunk_rows(number):
        return pl.ds(pl.multiple_of(number * CHUNK, CHUNK), CHUNK)

    def send_factors(condition, part, which, target_z, target_core):
        rows = pl.ds(which * (CHUNK // 2), CHUNK // 2)
        there = pl.ds(pl.multiple_of(row * CHUNK + which * (CHUNK // 2), CHUNK // 2), CHUNK // 2)

        @pl.when(condition)
        def _():
            for step in range(8):
                remote(factors.at[part, rows], fac.at[part, there], fac_sent, fac_got.at[part],
                       device(0, step, target_z, target_core)).start()

    def send_part(part):
        send_factors(fac_own, part, 0, z, 0)
        send_factors(fac_next, part, 1, z, 0)
        send_factors(fac_far, part, 0, z + 1, 1)
        send_factors(fac_off, part, 1, z + 1, 1)

    send_part(0)

    def scatter_copy(number):
        rows = pl.ds(number * CHUNK, CHUNK)
        at, level = relay_chip(number)
        return remote(cov.at[0, rows], lead.at[rows], one_sent.at[4], one_got.at[4], device(at, 1, level, number // 8))

    @pl.when(scatter)
    def _():
        for number in range(16):
            scatter_copy(number).start()

    side_panel = remote(cov.at[other], panel.at[core], one_sent.at[0], one_got.at[0], sibling)
    pl.when(home)(side_panel.start)
    send_part(1)

    @pl.when(relay)
    def _():
        rows = chunk_rows(relay_place)
        remote(lead.at[rows], lead.at[rows], one_sent.at[4], one_got.at[4], sibling).wait_recv()
        for number in range(16):
            remote(lead.at[rows], lead.at[rows], lead_sent, lead_got,
                   device(0, number % 8, number // 8 * 4, core)).start()

    def block_rows(number, start=0):
        return pl.ds(pl.multiple_of(start + number * BLOCK, BLOCK), BLOCK)

    def piece(index):
        return pl.ds(pl.multiple_of(index * PIECE, PIECE), PIECE)

    def half_piece(index, which):
        return pl.ds(pl.multiple_of(index * PIECE + which * HALF, HALF), HALF)

    def row_copy(index, sent, target):
        rows = piece(index)
        return remote(buf.at[core, rows], buf.at[core, rows], sent, row_got.at[index], target)

    def side_copy(index, slot):
        rows = piece(index)
        return remote(buf.at[slot, rows], buf.at[slot, rows], side_sent.at[slot], side_got.at[slot, index // (NP // 2)],
                      sibling)

    def source_copy(index, slot, place_to, sent, target):
        rows = piece(index)
        return remote(buf.at[slot, rows], buf.at[place_to, rows], sent, up_got.at[index], target)

    def tip_copy(index, which, got, target):
        rows = piece(index)
        return remote(buf.at[held, rows], buf.at[2, rows], tip_sent.at[which], got.at[index], target)

    def ring_copy(index, which, sent, got, target):
        rows = half_piece(index, which)
        return remote(buf.at[held, rows], buf.at[2, rows], sent, got.at[index], target)

    z_to = device(x, y, z + jnp.where(back, 7, 1), core)
    xp_to, xm_to = device(x + 1, y, z, core), device(x + 3, y, z, core)
    up_to, down_to = device(x, y + 1, z, core), device(x, y + 7, z, core)

    def send_row(index, to_side):
        def start(condition, copy):
            pl.when(condition)(copy.start)

        start(direct_out, source_copy(index, core, 2, direct_sent, direct_to))
        start(cross_out | cross_home, source_copy(index, core, 2, cross_sent, cross_to))
        start(z_child, row_copy(index, z_sent, z_to))
        start(xm_child, row_copy(index, xm_sent, xm_to))
        start(xp_child, row_copy(index, xp_sent, xp_to))
        start(to_side, side_copy(index, core))

    def side_wait(slot, part):
        total(TILE, side_sent.at[slot], side_got.at[slot, part]).wait_recv()

    def make_panel():
        part_rows = jnp.where(first, half, 1 - half) * 256
        tile_row = core * 16 + row
        side_fac, side_rows = [], pl.ds(pl.multiple_of(part_rows, 256), 256)
        for part in range(2):
            side_fac.append(remote(fac.at[part, side_rows], fac.at[part, side_rows],
                                   one_sent.at[1 + part], one_got.at[1 + part], sibling))
        lead_rows = pl.ds(pl.multiple_of(core * 256, 256), 256)
        side_lead = remote(lead.at[lead_rows], lead.at[lead_rows], one_sent.at[3], one_got.at[3], sibling)

        def split_into(at, load):
            def body(number, carry):
                rows = block_rows(number)
                wide[at, rows], narrow[at, rows] = split(load(rows))
                return carry

            lax.fori_loop(0, BLOCKS, body, 0)

        def send_block(number, start):
            def body(index, carry):
                root_send(start + number * GROUP + index)
                return carry

            lax.fori_loop(0, GROUP, body, 0)

        def root_send(index):
            copy = source_copy(index, 0, 0, direct_sent, device(0, y, turn, turn_core))
            pl.when(turn_out)(copy.start)
            send_row(index, False)

        total(8 * CHUNK, fac_sent, fac_got.at[0]).wait_recv()
        side_fac[0].start()
        band_copy.wait()
        row_band = band[tile_row]
        panel_copy.wait()
        side_panel.wait_recv()
        side_fac[0].wait_recv()
        split_into(0, lambda rows: fac[0, rows])
        kept = (tile_row > 0) & (tile_row <= row_band)

        def first_block(number, carry):
            rows = block_rows(number)
            left = split(jnp.where(kept, panel[0, rows], 0.0))
            buf[core, rows] = dot3(left, (wide[0], narrow[0]), False)
            send_block(number, 0)
            return carry

        lax.fori_loop(0, BLOCKS, first_block, 0)

        def turned_block(number, carry):
            rows = block_rows(number)
            made = dot3(split(buf[core, rows]), (wide[0], narrow[0]), True)
            wide[3, rows], narrow[3, rows] = split(made)
            return carry

        lax.fori_loop(0, BLOCKS, turned_block, 0)
        total(8 * CHUNK, fac_sent, fac_got.at[1]).wait_recv()
        side_fac[1].start()
        total(8 * CHUNK, lead_sent, lead_got).wait_recv()
        side_lead.start()
        side_fac[1].wait_recv()
        split_into(1, lambda rows: fac[1, rows])
        lead_kept = band[1] >= 1
        side_lead.wait_recv()
        split_into(2, lambda rows: jnp.where(lead_kept, lead[rows], 0.0))
        panel_kept = (tile_row > 0) & (tile_row - 1 <= row_band)

        def second_block(number, carry):
            rows = block_rows(number)
            update = dot3((wide[3, rows], narrow[3, rows]), (wide[2], narrow[2]), True)
            left = split(jnp.where(panel_kept, panel[1, rows], 0.0) - update)
            made = dot3(left, (wide[1], narrow[1]), False)
            buf[core, block_rows(number, TILE)] = jnp.where(tile_row > 1, made, 0.0)
            send_block(number, NP // 2)
            return carry

        lax.fori_loop(0, BLOCKS, second_block, 0)
        for part in range(2):
            rows = pl.ds(part * TILE, TILE)
            remote(buf.at[core, rows], buf.at[core, rows], side_sent.at[core], side_got.at[core, part], sibling).start()
        for part in range(2):
            side_wait(other, part)
        for s in range(2):
            def body(number, carry):
                rows = block_rows(number)
                out[s, rows] = buf[s, block_rows(number, core * TILE)]
                return carry

            lax.fori_loop(0, BLOCKS, body, 0)
        side_panel.wait_send()
        side_fac[0].wait_send()
        side_fac[1].wait_send()
        side_lead.wait_send()

        @pl.when(scatter)
        def _():
            total(16 * CHUNK, one_sent.at[4], one_got.at[4]).wait_send()

        pl.when(turn_out)(total(2 * TILE, direct_sent, one_got.at[0]).wait_send)

    def make_base():
        noise_copy.wait()
        morton_copy.wait()
        cov_copy.wait()
        band_copy.wait()
        diagonal = row == lax.rem(col, 16)
        for s in range(2):
            tile = s * 16 + row
            kept = (col <= tile) & (tile - col <= band[tile])
            on_diagonal = diagonal & (col // 16 == s)

            @pl.when(on_diagonal)
            def _():
                turned_noise = noise[...].T
                top = turned_noise.astype(BF16)
                rest = turned_noise - top.astype(F32)
                middle = rest.astype(BF16)
                bottom = (rest - middle.astype(F32)).astype(BF16)
                lanes = lax.broadcasted_iota(jnp.int32, (128, 128), 0)
                for number in range(BLOCKS):
                    stations = morton[pl.ds(tile * BLOCKS + number, 1), :]
                    upper, lower = stations // 128, stations % 128
                    pick = jnp.where(lanes == upper, 1.0, 0.0).astype(BF16)
                    found = jnp.dot(top, pick, preferred_element_type=F32)
                    found = found + (jnp.dot(middle, pick, preferred_element_type=F32)
                                     + jnp.dot(bottom, pick, preferred_element_type=F32))
                    nugget = jnp.sum(jnp.where(lanes == lower, found, 0.0), axis=0, keepdims=True)
                    at = number * BLOCK
                    rows_at = lax.broadcasted_iota(jnp.int32, (BLOCK, TILE), 0) + at
                    cols_at = lax.broadcasted_iota(jnp.int32, (BLOCK, TILE), 1)
                    value = jnp.where(cols_at <= rows_at, out[s, pl.ds(at, BLOCK), :], out[s, :, pl.ds(at, BLOCK)].T)
                    out[s, pl.ds(at, BLOCK), :] = value
                    corner = out[s, pl.ds(at, BLOCK), pl.ds(at, BLOCK)]
                    eye = lanes == lax.broadcasted_iota(jnp.int32, (128, 128), 1)
                    out[s, pl.ds(at, BLOCK), pl.ds(at, BLOCK)] = corner + jnp.where(eye, nugget, 0.0)

            @pl.when(jnp.logical_not(on_diagonal))
            def _():
                def body(number, carry):
                    rows = block_rows(number)
                    out[s, rows] = jnp.where(kept, out[s, rows], 0.0)
                    return carry

                lax.fori_loop(0, BLOCKS, body, 0)

    needed = [away & (col <= s * 16 + row) & (s * 16 + row <= 25) for s in range(2)]
    by_side = [
        away & either(second & either(high & (x == 0), low & (x == 0) & (zl >= 1) & (zl < turn), high & (x == 1) & (zl <= turn),
                                      low & (x == 0) & (zl == turn) & (turn_core == 0)),
                      first & low & (x == 0) & (zl == turn) & (turn_core == 1)),
        away & first & either(low & (x <= 2), tail & either(x <= 2, zl == 0)),
    ]

    def update_block(number):
        part, block = number // BLOCKS, number % BLOCKS

        @pl.when(block == 0)
        def _():
            for s in range(2):
                @pl.when(by_side[s])
                def _():
                    side_wait(s, part)

                @pl.when(needed[s])
                def _():
                    def body(index, carry):
                        rows = block_rows(index)
                        wide[s, rows], narrow[s, rows] = split(buf[s, block_rows(index, part * TILE)])
                        return carry

                    lax.fori_loop(0, BLOCKS, body, 0)

        right = split(buf[held, block_rows(number)])
        columns = pl.ds(pl.multiple_of(block * BLOCK, BLOCK), BLOCK)
        for s in range(2):
            @pl.when(needed[s])
            def _():
                out[s, :, columns] = out[s, :, columns] - dot3((wide[s], narrow[s]), right, True)

    row_delay = depth * ROW_HOP
    col_delay = lag * ROW_HOP
    last_delay = 3 * ROW_HOP
    arrival = jnp.where(ring, col_delay + COL_HOP * jnp.where(here, 0, jnp.maximum(place, 8 - place)), last_delay)
    uses = by_side[0] | turning | (first & row_in), by_side[1] | (second & row_in)
    rows_from = ROW_HOP * jnp.maximum(jnp.where(uses[0], depths[0], 0), jnp.where(uses[1], depths[1], 0))
    update_delay = jnp.maximum(arrival, rows_from + SLACK + NP // 2 - GROUP + 1)

    def inside(index):
        return (index >= 0) & (index < NP)

    def in_bulk(index):
        return (index >= 0) & (index < BULK)

    def step(time, carry):
        index = time - row_delay

        @pl.when(row_in & inside(index))
        def _():
            row_copy(index, z_sent, z_to).wait_recv()
            send_row(index, side_out)

        ahead = time - col_delay

        @pl.when(source & inside(ahead))
        def _():
            pl.when(jnp.logical_not(own_row))(source_copy(ahead, 2, 2, up_sent, up_to).wait_recv)

            @pl.when(ahead < BULK)
            def _():
                ring_copy(ahead, 0, up_sent, up_got, up_to).start()
                ring_copy(ahead, 1, down_sent, down_got, down_to).start()

            @pl.when(ahead >= BULK)
            def _():
                tip_copy(ahead, 0, up_got, up_to).start()
                tip_copy(ahead, 1, down_got, down_to).start()

            pl.when(jump_out)(source_copy(ahead, 2, 2, cross_sent, device(2, y, 4, core)).start)

            @pl.when(turning)
            def _():
                side_copy(ahead, 0).start()

                @pl.when(zl >= 2)
                def _():
                    rows = piece(ahead)
                    remote(buf.at[0, rows], buf.at[0, rows], direct_sent, row_got.at[ahead], device(0, y, z + 7, 0)).start()

        going_up = ahead - COL_HOP * place
        going_down = ahead - COL_HOP * (8 - place)
        straight = time - last_delay

        @pl.when(last_in & inside(straight))
        def _():
            source_copy(straight, 2, 2, up_sent, up_to).wait_recv()

        @pl.when(follower & (place <= 4) & (going_up >= BULK) & (going_up < NP))
        def _():
            copy = tip_copy(going_up, 0, up_got, up_to)
            copy.wait_recv()
            pl.when(place <= 3)(copy.start)

        @pl.when(follower & (place >= 5) & (going_down >= BULK) & (going_down < NP))
        def _():
            copy = tip_copy(going_down, 1, down_got, down_to)
            copy.wait_recv()
            pl.when(place >= 6)(copy.start)

        @pl.when(follower & in_bulk(going_up))
        def _():
            copy = ring_copy(going_up, 0, up_sent, up_got, up_to)
            copy.wait_recv()
            pl.when(place <= 6)(copy.start)

        @pl.when(follower & in_bulk(going_down))
        def _():
            copy = ring_copy(going_down, 1, down_sent, down_got, down_to)
            copy.wait_recv()
            pl.when(place >= 2)(copy.start)

        done = time - update_delay + 1

        @pl.when((done > 0) & (done % GROUP == 0) & (done <= NP))
        def _():
            update_block(done // GROUP - 1)

        return carry

    def drain(condition, rows, sent):
        pl.when(condition)(total(rows, sent, one_got.at[0]).wait_send)

    pl.when(home)(make_panel)

    @pl.when(away)
    def _():
        make_base()
        lax.fori_loop(0, update_delay + NP, step, 0)

    drain(z_child, 2 * TILE, z_sent)
    drain(xp_child, 2 * TILE, xp_sent)
    drain(xm_child, 2 * TILE, xm_sent)
    drain(cross_out | cross_home | jump_out, 2 * TILE, cross_sent)
    drain(direct_out | (turning & (zl >= 2)), 2 * TILE, direct_sent)
    drain(send_up, BULK * HALF, up_sent)
    drain(send_down, BULK * HALF, down_sent)
    drain(tip_up, TIP * PIECE, tip_sent.at[0])
    drain(tip_down, TIP * PIECE, tip_sent.at[1])
    for s in range(2):
        drain(either((home | side_out) & (core == s), turning & (s == 0)), 2 * TILE, side_sent.at[s])
    drain(either(fac_own, fac_far, fac_next, fac_off), 8 * CHUNK, fac_sent)
    drain(relay, 16 * CHUNK, lead_sent)


def on_device(cov_tiles, inverse_factors, band, station_noise, morton):
    vmem = pl.BlockSpec(memory_space=pltpu.VMEM)
    hbm = pl.BlockSpec(memory_space=pltpu.HBM)
    dma = pltpu.SemaphoreType.DMA
    out = pl.pallas_call(
        kernel,
        out_shape=jax.ShapeDtypeStruct((2, TILE, TILE), F32),
        in_specs=[hbm] * 5,
        out_specs=vmem,
        scratch_shapes=[
            pltpu.VMEM((3, 2 * TILE, TILE), F32),
            pltpu.VMEM((2, TILE, TILE), F32),
            pltpu.VMEM((2, TILE, TILE), F32),
            pltpu.VMEM((TILE, TILE), F32),
            pltpu.VMEM((4, TILE, TILE), BF16),
            pltpu.VMEM((4, TILE, TILE), BF16),
            pltpu.SMEM((32,), jnp.int32),
            pltpu.VMEM((128, 128), F32),
            pltpu.VMEM((128, 128), jnp.int32),
            dma((NP,)), dma((NP,)), dma((NP,)), dma((2, 2)), dma((2,)), dma, dma((5,)),
            dma, dma, dma, dma, dma, dma, dma, dma((2,)), dma, dma, dma((5,)),
            dma((2,)), dma((5,)),
        ],
        compiler_params=pltpu.CompilerParams(
            collective_id=0, has_side_effects=True, vmem_limit_bytes=40 * 1024 * 1024
        ),
        cost_estimate=pl.CostEstimate(flops=6 * 4 * 2 * TILE**3, bytes_accessed=4 * 1024 * 1024, transcendentals=0),
        name="panel_steps",
    )(
        *(
            pltpu.with_memory_space_constraint(operand, pltpu.HBM)
            for operand in (
                cov_tiles.reshape(2, TILE, TILE),
                inverse_factors,
                band,
                station_noise.reshape(128, 128),
                morton.reshape(128, 128),
            )
        )
    )
    return out.reshape(cov_tiles.shape)


def solution(mesh):
    placed = (P(None, "row", None, "col", None, None), P(None, "row", None), P(), P(), P())
    return jax.shard_map(
        on_device,
        mesh=mesh,
        in_specs=placed,
        out_specs=P(None, "row", None, "col", None, None),
        check_vma=False,
    )
```
